256 devices in a mesh: frame: 8 (over y, z_lo), head: 16 (over x, z_hi), tok: 2 (over core).
Axes of the slice: x: 4, y: 4, z: 8 (z_hi: 4, z_lo: 2; z = z_hi * 2 + z_lo), core: 2. Of those that a mesh axis runs over, the one named last changes fastest.
Arguments:
- queue: bfloat16 [16, 1024, 3072], P('frame', ('head', 'tok')), may hold values from -6 to 6
- timesteps: int32 [16], P('frame'), may hold values from 0 to 49
- mod_table: float32 [50, 3, 3072], replicated, may hold values from -3 to 3
- w_qkv: bfloat16 [3072, 16, 384], P(None, 'head'), may hold values from -0.108253175 to 0.108253175
- norm_gains: float32 [2, 128], replicated, may hold values from 0.7 to 4
- w_out: bfloat16 [16, 128, 3072], P('head'), may hold values from -0.125 to 0.125
- noise_frame: bfloat16 [1024, 3072], P(('head', 'tok')), may hold values from -6 to 6
Outputs:
- queue_next: bfloat16 [16, 1024, 3072], P('frame', ('head', 'tok'))
The draws below stay inside these ranges and needn't reach their ends.
All inputs are finite; a program needn't handle non-finite values.
Results may differ from the reference program's by a relative error of at most 0.012.
Values may be sent and summed in bfloat16 or wider, within the bound.
A program may use at most 64 MiB of HBM per device.

```python
import jax
import jax.numpy as jnp
from jax import lax

D = 3072
HS = 128
HEADS = 16
STEPS = 50
F = 16
S = 1024


def draw_w_qkv(key, part):
    key = jax.random.fold_in(key, 11)
    key_q, key_k, key_v = jax.random.split(key, 3)
    scale = D ** (-0.5)
    first = jax.random.normal(key_q, (D, HEADS, HS), jnp.float32)
    second = jax.random.normal(key_k, (D, HEADS, HS), jnp.float32)
    third = jax.random.normal(key_v, (D, HEADS, HS), jnp.float32)
    whole = jnp.concatenate([first, second, third], axis=-1) * scale
    return jnp.clip(whole, -6.0 * scale, 6.0 * scale).astype(jnp.bfloat16)


def draw_norm_gains(key, part):
    key = jax.random.fold_in(key, 17)
    return jax.random.uniform(key, (2, HS), jnp.float32, 0.7, 1.6)


def touch_ends(array, own_key, smallest, top_value):
    place = [jax.random.randint(jax.random.fold_in(own_key, axis), (), 0, length) for axis, length in enumerate(array.shape)]
    longest = array.shape.index(max(array.shape))
    next_to = place[:longest] + [(place[longest] + 1) % array.shape[longest]] + place[longest + 1:]
    return array.at[tuple(place)].set(smallest).at[tuple(next_to)].set(top_value)


def block_levels(key, dims, cuts, least, top_value):
    def one(dim, parts):
        steps = jax.random.uniform(jax.random.fold_in(jax.random.fold_in(key, 6), dim), (parts,), jnp.float32, least / len(cuts), top_value / len(cuts))
        return jnp.repeat(jnp.exp(steps), dims[dim] // parts).reshape((-1,) + (1,) * (len(dims) - dim - 1))

    loudness = one(*cuts[0])
    for cut in cuts[1:]:
        loudness = loudness * one(*cut)
    return loudness


def noise(stream_key, extent, scale, bound, cuts=(), kind=jnp.bfloat16):
    loudness = block_levels(stream_key, extent, cuts, -0.22, 0.18) if cuts else 1.0
    entries = jax.random.normal(stream_key, extent, jnp.float32) * scale * loudness
    return jnp.minimum(jnp.maximum(entries, -bound), bound).astype(kind)


def setup_inputs(seed: int = 0) -> dict:
    splits = jax.random.split(jax.random.key(seed), 8)
    return {
        "queue": noise(splits[0], (F, S, D), 1.0, 6.0, ((0, 8), (1, 32))),
        "timesteps": touch_ends(jax.random.randint(splits[1], (F,), 0, STEPS), jax.random.fold_in(splits[1], 1), 0, STEPS - 1).astype(jnp.int32),
        "mod_table": noise(splits[2], (STEPS, 3, D), 0.5, 3.0, (), jnp.float32),
        "w_qkv": draw_w_qkv(jax.random.fold_in(splits[7], 71), 0),
        "norm_gains": draw_norm_gains(jax.random.fold_in(splits[7], 71), 0),
        "w_out": noise(splits[5], (HEADS, HS, D), (HEADS * HS) ** -0.5, 0.125, ((0, 16),)),
        "noise_frame": noise(splits[6], (S, D), 1.0, 6.0, ((0, 32),)),
    }


def rms_scale(values, gain):
    return values * lax.rsqrt(lax.optimization_barrier(jnp.mean(values * values, axis=-1, keepdims=True)) + 1e-06) * gain

def reference(queue, timesteps, mod_table, w_qkv, norm_gains, w_out, noise_frame):
    frames = queue.shape[0]
    tokens = queue.shape[1]
    width = queue.shape[2]
    onehot = (timesteps[:, None] == jnp.arange(STEPS, dtype=jnp.int32)[None, :]).astype(jnp.float32)
    mods = jnp.einsum('fs,scd->fcd', onehot, mod_table, precision=lax.Precision.HIGHEST)
    shift_v, scale_v, gate_v = (mods[:, 0], mods[:, 1], mods[:, 2])
    xfull = queue.astype(jnp.float32)
    mean = lax.optimization_barrier(jnp.mean(xfull, axis=-1, keepdims=True))
    centred = xfull - mean
    normed = centred * lax.rsqrt(lax.optimization_barrier(jnp.mean(centred * centred, axis=-1, keepdims=True)) + 1e-06)
    modulated = (normed * (1.0 + scale_v[:, None, :]) + shift_v[:, None, :]).astype(jnp.bfloat16)
    flat = modulated.reshape(frames * tokens, width)
    inv_scale = 1.0 / jnp.sqrt(jnp.float32(HS))

    def head_step(head, total):
        weight = lax.dynamic_index_in_dim(w_qkv, head, 1, keepdims=False)
        qkv = jnp.dot(flat, weight, preferred_element_type=jnp.float32)
        query = rms_scale(qkv[:, :HS], norm_gains[0]).astype(jnp.bfloat16).reshape(frames, tokens, HS)
        keys = rms_scale(qkv[:, HS:2 * HS], norm_gains[1]).astype(jnp.bfloat16).reshape(frames, tokens, HS)
        values = qkv[:, 2 * HS:].astype(jnp.bfloat16).reshape(frames, tokens, HS)
        padded_k = jnp.pad(keys, ((1, 1), (0, 0), (0, 0)))
        padded_v = jnp.pad(values, ((1, 1), (0, 0), (0, 0)))

        def frame_attend(slot):
            key_rows = lax.dynamic_slice_in_dim(padded_k, slot, 3, 0).reshape(3 * tokens, HS)
            val_rows = lax.dynamic_slice_in_dim(padded_v, slot, 3, 0).reshape(3 * tokens, HS)
            global_frame = slot - 1 + jnp.arange(3, dtype=jnp.int32)
            valid = jnp.repeat((global_frame >= 0) & (global_frame < frames), tokens)
            rows = lax.dynamic_index_in_dim(query, slot, 0, keepdims=False)
            scores = jnp.dot(rows, key_rows.T, preferred_element_type=jnp.float32) * inv_scale
            scores = jnp.where(valid[None, :], scores, -1e+30)
            peak = lax.optimization_barrier(jnp.max(scores, axis=-1, keepdims=True))
            probs = jnp.exp(scores - peak)
            total_p = lax.optimization_barrier(jnp.sum(probs, axis=-1, keepdims=True))
            mixed = jnp.dot(probs.astype(jnp.bfloat16), val_rows, preferred_element_type=jnp.float32)
            return (mixed / total_p).astype(jnp.bfloat16)
        attn = lax.map(frame_attend, jnp.arange(frames, dtype=jnp.int32))
        out_weight = lax.dynamic_index_in_dim(w_out, head, 0, keepdims=False)
        contrib = jnp.dot(attn.reshape(frames * tokens, HS), out_weight, preferred_element_type=jnp.float32)
        contrib = lax.optimization_barrier(contrib.astype(jnp.bfloat16)).astype(jnp.float32)
        return total + contrib
    proj = lax.fori_loop(0, w_qkv.shape[1], head_step, jnp.zeros((frames * tokens, width), jnp.float32))
    proj = proj.reshape(frames, tokens, width)
    block_out = (xfull + gate_v[:, None, :] * proj).astype(jnp.bfloat16)
    return jnp.concatenate([noise_frame[None], block_out[:-1]], axis=0)
```

```python
import functools

import jax
import jax.numpy as jnp
from jax import lax
from jax.experimental import pallas as pl
from jax.experimental.pallas import tpu as pltpu
from jax.sharding import PartitionSpec as P

MESH = pl.DeviceIdType.MESH
NX = 4
NY = 4
NZ = 4
OWN, LEFT, RIGHT, OPP = 0, 1, 2, 3


class Place:
    def __init__(self):
        self.frame = lax.axis_index("frame")
        self.head = lax.axis_index("head")
        self.core = lax.axis_index("tok")
        self.x, self.zh = self.head // NZ, self.head % NZ
        self.y, self.zl = self.frame // 2, self.frame % 2

    def to(self, x=0, z=0, y=0, frame=0, flip=False, core=None):
        head = ((self.x + x) % NX) * NZ + (self.zh + z) % NZ
        own = ((self.y + y) % NY) * 2 + self.zl if frame == 0 else self.frame + frame
        tok = self.core if core is None else core
        tok = 1 - tok if flip else tok
        return (own, head, tok)


class Copies:
    def __init__(self, send, recv):
        self.send, self.recv, self.count, self.all = send, recv, 0, {}

    def make(self, name, src, dst, device):
        k = self.count
        self.count += 1
        copy = pltpu.make_async_remote_copy(
            src_ref=src,
            dst_ref=dst,
            send_sem=self.send.at[k],
            recv_sem=self.recv.at[k],
            device_id=device,
            device_id_type=MESH,
        )
        self.all[name] = copy
        return copy

    def start(self, name, src, dst, device):
        self.make(name, src, dst, device).start()

    def got(self, *names):
        for name in names:
            self.all[name].wait_recv()

    def sent(self, skip=()):
        for name, copy in self.all.items():
            if name not in skip:
                copy.wait_send()


def greet(devices, count):
    barrier = pltpu.get_barrier_semaphore()
    for device in devices:
        pl.semaphore_signal(barrier, inc=1, device_id=device, device_id_type=MESH)
    pl.semaphore_wait(barrier, count)


class Gather:
    def __init__(self, tag, copies, me, ring, source, held, half):
        self.tag, self.copies, self.me, self.ring = tag, copies, me, ring
        self.source, self.held, self.half = source, held, half
        self.mine = me.core * NY + me.y
        self.left = me.core * NY + (me.y + NY - 1) % NY
        self.right = me.core * NY + (me.y + 1) % NY
        self.far = me.core * NY + (me.y + 2) % NY

    def part(self, rel, eighth, which):
        return self.half(self.held, rel, eighth, which)

    def go(self, name, src, dst, device):
        self.copies.start(self.tag + name, src, dst, device)

    def got(self, *names):
        self.copies.got(*[self.tag + name for name in names])

    def ring_start(self):
        e = self.mine
        self.go("r", self.source.at[e], self.held.at[LEFT, e], self.me.to(**{self.ring: 1}))
        self.go("l", self.source.at[e], self.held.at[RIGHT, e], self.me.to(**{self.ring: -1}))

    def ring_relay(self):
        e = self.mine
        self.got("r")
        self.go("rr", self.part(LEFT, e, 0), self.part(OPP, e, 0), self.me.to(**{self.ring: 1}))
        self.y_start(LEFT)
        self.got("l")
        self.go("ll", self.part(RIGHT, e, 1), self.part(OPP, e, 1), self.me.to(**{self.ring: -1}))
        self.y_start(RIGHT)

    def ring_end(self):
        self.got("rr", "ll")
        self.y_start(OPP)

    def y_start(self, rel):
        n, e = str(rel), self.mine
        self.go("yr" + n, self.held.at[rel, e], self.held.at[rel, e], self.me.to(y=1))
        self.go("yl" + n, self.held.at[rel, e], self.held.at[rel, e], self.me.to(y=-1))
        self.go("s0" + n, self.held.at[rel, e], self.held.at[rel, e], self.me.to(flip=True))

    def y_relay(self, rel):
        n = str(rel)
        self.got("yr" + n)
        e = self.left
        self.go("yrr" + n, self.part(rel, e, 0), self.part(rel, e, 0), self.me.to(y=1))
        self.go("s1" + n, self.held.at[rel, e], self.held.at[rel, e], self.me.to(flip=True))
        self.got("yl" + n)
        e = self.right
        self.go("yll" + n, self.part(rel, e, 1), self.part(rel, e, 1), self.me.to(y=-1))
        self.go("s2" + n, self.held.at[rel, e], self.held.at[rel, e], self.me.to(flip=True))

    def y_end(self, rel):
        n = str(rel)
        self.got("yrr" + n, "yll" + n)
        e = self.far
        self.go("s3" + n, self.held.at[rel, e], self.held.at[rel, e], self.me.to(flip=True))

    def done(self, rel):
        n = str(rel)
        self.got("s0" + n, "s1" + n, "s2" + n, "s3" + n)


def rms_scale(values, gain):
    return values * lax.rsqrt(jnp.mean(values * values, axis=-1, keepdims=True) + 1e-06) * gain


def qkv_kernel(
    steps_ref, mod_hbm, queue_ref, w_hbm, gains_ref, q_out, kv_out,
    mod, xg, wg, sb, rb, local, send, recv,
):
    me = Place()
    core = me.core
    rows = queue_ref.shape[1]
    width = queue_ref.shape[2]
    hs = gains_ref.shape[1]
    partners = [me.to(flip=True)]
    for shift in (1, -1, 2):
        partners += [me.to(x=shift), me.to(x=shift, flip=True)]
    for shift in (1, -1):
        partners += [me.to(z=shift), me.to(y=shift)]
    mod_copy = pltpu.make_async_copy(mod_hbm, mod, local.at[0])
    mod_copy.start()
    own_copy = pltpu.make_async_copy(w_hbm, wg.at[OWN], local.at[1])
    own_copy.start()
    greet(partners, len(partners))

    copies = Copies(send, recv)
    seg = wg.shape[2] // 2
    weights = Gather(
        "w", copies, me, "x", w_hbm, wg,
        lambda ref, rel, e, which: ref.at[rel, e, pl.ds(which * seg, seg)],
    )
    weights.ring_start()

    mod_copy.wait()
    for slot in range(2):
        level = steps_ref[slot]
        x = queue_ref[slot].astype(jnp.float32)
        centred = x - jnp.mean(x, axis=-1, keepdims=True)
        normed = centred * lax.rsqrt(jnp.mean(centred * centred, axis=-1, keepdims=True) + 1e-06)
        mods = mod[level]
        xg[OWN, slot * rows : (slot + 1) * rows, :] = (
            normed * (1.0 + mods[1:2, :]) + mods[0:1, :]
        ).astype(jnp.bfloat16)
    copies.start("zr", xg.at[OWN], xg.at[LEFT], me.to(z=1))
    copies.start("zl", xg.at[OWN], xg.at[RIGHT], me.to(z=-1))

    weights.ring_relay()
    weights.ring_end()
    weights.y_relay(LEFT)
    copies.got("zr")
    copies.start("zrr", xg.at[LEFT, pl.ds(0, rows)], xg.at[OPP, pl.ds(0, rows)], me.to(z=1))
    copies.got("zl")
    copies.start("zll", xg.at[RIGHT, pl.ds(rows, rows)], xg.at[OPP, pl.ds(rows, rows)], me.to(z=-1))
    weights.y_relay(RIGHT)
    weights.y_end(LEFT)
    weights.y_relay(OPP)
    weights.y_end(RIGHT)
    copies.got("zrr", "zll")
    own_copy.wait()

    fold = jnp.float32(1.4426950408889634 / hs**0.5)
    tokens = NZ * rows

    def project(rel):
        xs = xg[...].reshape(NZ * 2 * rows, width)
        w = wg[rel].reshape(width, 3 * hs)
        qkv = jnp.dot(xs, w, preferred_element_type=jnp.float32)
        q = rms_scale(qkv[:, :hs], gains_ref[0:1, :] * fold)
        k = rms_scale(qkv[:, hs : 2 * hs], gains_ref[1:2, :])
        out = jnp.concatenate([q, k, qkv[:, 2 * hs :]], axis=-1).astype(jnp.bfloat16)
        out = out.reshape(NZ, 2, rows, 3 * hs)
        for slot in range(2):
            sb[rel, slot] = out[:, slot].reshape(tokens, 3 * hs)

    back = {LEFT: RIGHT, RIGHT: LEFT, OPP: OPP}
    shift = {LEFT: -1, RIGHT: 1, OPP: 2}
    project(OWN)
    copies.start("a0", sb.at[OWN, 1 - core], rb.at[OWN, core], me.to(flip=True))
    rb[OWN, core] = sb[OWN, core]
    for rel in (LEFT, RIGHT, OPP):
        if rel == OPP:
            weights.y_end(OPP)
        weights.done(rel)
        project(rel)
        n = str(rel)
        copies.start("a" + n, sb.at[rel, core], rb.at[back[rel], core], me.to(x=shift[rel]))
        copies.start(
            "b" + n, sb.at[rel, 1 - core], rb.at[back[rel], core], me.to(x=shift[rel], flip=True)
        )
    copies.got("a0")
    for rel in (LEFT, RIGHT, OPP):
        copies.got("a" + str(rel), "b" + str(rel))
    all_rows = rb[...].reshape(NX * 2 * tokens, 3 * hs)
    q_out[...] = all_rows[:, :hs]
    kv_out[...] = all_rows[:, hs:]
    copies.sent()


def out_kernel(
    steps_ref, mod_hbm, queue_ref, noise_ref, q_ref, kv_ref, w_hbm, out_ref,
    mod, kvb, kt, vx, oa, top, attn_s, attn_g, wo, po, pl_s, pr_s, rl, rr, fl, fr, qb, ob, ou,
    local, send, recv,
):
    me = Place()
    core, frame = me.core, me.frame
    frames = lax.axis_size("frame")
    hs = q_ref.shape[1]
    rows = queue_ref.shape[1]
    width = queue_ref.shape[2]
    keys = kv_ref.shape[0]
    half = width // 2
    chunk = keys // NX
    step = 2 * core - 1
    beside = frame + step
    has_beside = jnp.logical_and(beside >= 0, beside < frames)
    after = (frame + 1) % frames
    before = (frame + frames - 1) % frames

    mod_copy = pltpu.make_async_copy(mod_hbm, mod, local.at[0])
    mod_copy.start()
    own_copy = pltpu.make_async_copy(w_hbm, wo.at[OWN], local.at[1])
    own_copy.start()
    partners = [me.to(flip=True)]
    for shift in (1, -1):
        partners += [me.to(x=shift), me.to(z=shift), me.to(y=shift)]
    partners += [me.to(z=2)]
    partners += [(before, me.head, 1)]
    barrier = pltpu.get_barrier_semaphore()
    for device in partners:
        pl.semaphore_signal(barrier, inc=1, device_id=device, device_id_type=MESH)

    @pl.when(core == 1)
    def _():
        for tok in range(2):
            pl.semaphore_signal(
                barrier, inc=1, device_id=(after, me.head, tok), device_id_type=MESH
            )

    pl.semaphore_wait(barrier, len(partners) + 2 * core)

    copies = Copies(send, recv)
    side = copies.make("kv", kv_ref, kvb.at[1], (beside, me.head, 1 - core))
    copies.start("ks", kv_ref, kvb.at[0], me.to(flip=True))

    @pl.when(has_beside)
    def _():
        side.start()

    copies.start("qs", queue_ref.at[1 - core], qb.at[core], me.to(flip=True))
    weights = Gather(
        "w", copies, me, "z", w_hbm, wo,
        lambda ref, rel, e, which: ref.at[rel, e, :, pl.ds(which * half, half)],
    )
    weights.ring_start()

    def take(which, ref):
        kt[which] = ref[:, :hs].T
        vx[which, :, :hs] = ref[:, hs:]
        vx[which, :, hs:] = jnp.ones((keys, hs), jnp.bfloat16)

    take(0, kv_ref)
    weights.ring_relay()
    weights.ring_end()
    copies.got("ks")
    take(1, kvb.at[0])

    block = 128

    @pl.loop(0, keys // block)
    def _(i):
        at = pl.ds(pl.multiple_of(i * block, block), block)
        q = q_ref[at, :]
        scores = [jnp.dot(q, kt[j], preferred_element_type=jnp.float32) for j in range(2)]
        peak = jnp.maximum(
            jnp.max(scores[0], axis=-1, keepdims=True), jnp.max(scores[1], axis=-1, keepdims=True)
        )
        total = jnp.zeros((block, 2 * hs), jnp.float32)
        for j in range(2):
            p = jnp.exp2(scores[j] - peak).astype(jnp.bfloat16)
            total += jnp.dot(p, vx[j], preferred_element_type=jnp.float32)
        oa[at, :] = total
        top[at, :] = jnp.broadcast_to(peak, (block, hs))

    for rel in (LEFT, RIGHT, OPP):
        weights.y_relay(rel)

    @pl.when(has_beside)
    def _():
        side.wait_recv()
        take(2, kvb.at[1])

        @pl.loop(0, keys // block)
        def _(i):
            at = pl.ds(pl.multiple_of(i * block, block), block)
            q = q_ref[at, :]
            s = jnp.dot(q, kt[2], preferred_element_type=jnp.float32)
            old = top[at, :]
            peak = jnp.maximum(old[:, :1], jnp.max(s, axis=-1, keepdims=True))
            p = jnp.exp2(s - peak).astype(jnp.bfloat16)
            scale = jnp.exp2(old[:, :1] - peak)
            oa[at, :] = oa[at, :] * scale + jnp.dot(p, vx[2], preferred_element_type=jnp.float32)

    back = {LEFT: RIGHT, RIGHT: LEFT, OPP: OPP}
    shift = {LEFT: -1, RIGHT: 1, OPP: 2}
    for rx in (OPP, RIGHT, LEFT, OWN):
        o = oa[rx * chunk : (rx + 1) * chunk, :]
        attn = (o[:, :hs] / o[:, hs:]).astype(jnp.bfloat16).reshape(2, NZ, rows, hs)
        attn_g[rx, OWN] = attn[:, OWN].reshape(2 * rows, hs)
        for rz in (LEFT, RIGHT, OPP):
            attn_s[rx, rz] = attn[:, rz].reshape(2 * rows, hs)
            copies.start(
                f"a{rx}{rz}", attn_s.at[rx, rz], attn_g.at[rx, back[rz]], me.to(z=shift[rz])
            )
    for rel in (LEFT, RIGHT, OPP):
        weights.y_end(rel)
    for rel in (LEFT, RIGHT, OPP):
        weights.done(rel)
    own_copy.wait()

    def contribution(rx):
        copies.got(*[f"a{rx}{rz}" for rz in (LEFT, RIGHT, OPP)])
        a = jnp.concatenate([attn_g[rx, rz] for rz in range(NZ)], axis=-1)
        return jnp.dot(a, wo[...].reshape(NZ * hs, width), preferred_element_type=jnp.float32)

    po[...] = contribution(OPP).astype(jnp.bfloat16)
    copies.start("rl", po.at[:, pl.ds(0, half)], rl, me.to(x=1))
    copies.start("rr", po.at[:, pl.ds(half, half)], rr, me.to(x=-1))

    p = contribution(RIGHT)
    pr_s[1] = p[:, half:].astype(jnp.bfloat16)
    copies.start("fl1", pr_s.at[1], fl.at[1], me.to(x=1))
    copies.got("rl")
    pr_s[0] = (p[:, :half] + rl[...].astype(jnp.float32)).astype(jnp.bfloat16)
    copies.start("fl0", pr_s.at[0], fl.at[0], me.to(x=1))

    p = contribution(LEFT)
    pl_s[0] = p[:, :half].astype(jnp.bfloat16)
    copies.start("fr0", pl_s.at[0], fr.at[0], me.to(x=-1))
    copies.got("rr")
    pl_s[1] = (p[:, half:] + rr[...].astype(jnp.float32)).astype(jnp.bfloat16)
    copies.start("fr1", pl_s.at[1], fr.at[1], me.to(x=-1))

    p = contribution(OWN)
    mod_copy.wait()
    copies.got("qs")
    qb[core] = queue_ref[core]
    gate = mod[steps_ref[core]][2:3, :]
    copies.got("fl1", "fr0", "fl0", "fr1")
    for h in range(2):
        cols = slice(h * half, (h + 1) * half)
        proj = p[:, cols] + fl[h].astype(jnp.float32) + fr[h].astype(jnp.float32)
        for tok in range(2):
            ob[tok, :, cols] = (
                qb[tok, :, cols].astype(jnp.float32)
                + gate[:, cols] * proj[tok * rows : (tok + 1) * rows]
            ).astype(jnp.bfloat16)

    near = copies.make("o1", ob.at[1], ou.at[1], me.to(flip=True))
    next0 = copies.make("n0", ob.at[0], ou.at[0], (after, me.head, 0))
    k = copies.count
    next1 = pltpu.make_async_remote_copy(
        src_ref=ob.at[1], dst_ref=ou.at[0], send_sem=send.at[k], recv_sem=recv.at[k - 1],
        device_id=(after, me.head, 1), device_id_type=MESH,
    )

    @pl.when(core == 0)
    def _():
        near.start()
        out_ref[1] = ob[0]
        near.wait_send()

    sends_on = jnp.logical_and(core == 1, frame < frames - 1)

    @pl.when(sends_on)
    def _():
        next0.start()
        next1.start()

    @pl.when(core == 1)
    def _():
        near.wait_recv()
        out_ref[1] = ou[1]

    @pl.when(frame == 0)
    def _():
        out_ref[0] = noise_ref[...]

    @pl.when(frame > 0)
    def _():
        next0.wait_recv()
        out_ref[0] = ou[0]

    @pl.when(sends_on)
    def _():
        next0.wait_send()
        next1.wait_send()

    @pl.when(has_beside)
    def _():
        side.wait_send()

    copies.sent(skip=("kv", "o1", "n0"))


def body(queue, timesteps, mod_table, w_qkv, norm_gains, w_out, noise_frame):
    slots, rows, width = queue.shape
    hs = w_out.shape[1]
    bf16, f32 = jnp.bfloat16, jnp.float32
    vmem = pl.BlockSpec(memory_space=pltpu.VMEM)
    hbm = pl.BlockSpec(memory_space=pl.ANY)
    smem = pl.BlockSpec(memory_space=pltpu.SMEM)
    tokens = NZ * rows
    keys = NX * 2 * tokens
    eighth = width // 8
    limit = 56 * 1024 * 1024
    q, kv = pl.pallas_call(
        qkv_kernel,
        out_shape=(
            jax.ShapeDtypeStruct((keys, hs), bf16),
            jax.ShapeDtypeStruct((keys, 2 * hs), bf16),
        ),
        in_specs=[smem, hbm, vmem, hbm, vmem],
        out_specs=(vmem, vmem),
        scratch_shapes=[
            pltpu.VMEM(mod_table.shape, f32),
            pltpu.VMEM((NZ, 2 * rows, width), bf16),
            pltpu.VMEM((NX, 8, eighth, 3 * hs), bf16),
            pltpu.VMEM((NX, 2, tokens, 3 * hs), bf16),
            pltpu.VMEM((NX, 2, tokens, 3 * hs), bf16),
            pltpu.SemaphoreType.DMA((2,)),
            pltpu.SemaphoreType.DMA((48,)),
            pltpu.SemaphoreType.DMA((48,)),
        ],
        compiler_params=pltpu.CompilerParams(
            collective_id=0, has_side_effects=True, vmem_limit_bytes=limit
        ),
        name="qkv",
    )(timesteps, mod_table, queue, w_qkv.reshape(8, eighth, 3 * hs), norm_gains)
    half = width // 2
    return pl.pallas_call(
        out_kernel,
        out_shape=jax.ShapeDtypeStruct(queue.shape, bf16),
        in_specs=[smem, hbm, vmem, vmem, vmem, vmem, hbm],
        out_specs=vmem,
        scratch_shapes=[
            pltpu.VMEM(mod_table.shape, f32),
            pltpu.VMEM((2, keys, 2 * hs), bf16),
            pltpu.VMEM((3, hs, keys), bf16),
            pltpu.VMEM((3, keys, 2 * hs), bf16),
            pltpu.VMEM((keys, 2 * hs), f32),
            pltpu.VMEM((keys, hs), f32),
            pltpu.VMEM((NX, NZ, 2 * rows, hs), bf16),
            pltpu.VMEM((NX, NZ, 2 * rows, hs), bf16),
            pltpu.VMEM((NZ, 8, hs // 8, width), bf16),
            pltpu.VMEM((2 * rows, width), bf16),
            pltpu.VMEM((2, 2 * rows, half), bf16),
            pltpu.VMEM((2, 2 * rows, half), bf16),
            pltpu.VMEM((2 * rows, half), bf16),
            pltpu.VMEM((2 * rows, half), bf16),
            pltpu.VMEM((2, 2 * rows, half), bf16),
            pltpu.VMEM((2, 2 * rows, half), bf16),
            pltpu.VMEM((2, rows, width), bf16),
            pltpu.VMEM((2, rows, width), bf16),
            pltpu.VMEM((2, rows, width), bf16),
            pltpu.SemaphoreType.DMA((2,)),
            pltpu.SemaphoreType.DMA((64,)),
            pltpu.SemaphoreType.DMA((64,)),
        ],
        compiler_params=pltpu.CompilerParams(
            collective_id=1, has_side_effects=True, vmem_limit_bytes=limit
        ),
        name="attend",
    )(timesteps, mod_table, queue, noise_frame, q, kv, w_out.reshape(8, hs // 8, width))


def solution(mesh):
    return jax.shard_map(
        body,
        mesh=mesh,
        in_specs=(
            P("frame", ("head", "tok"), None),
            P("frame"),
            P(),
            P(None, "head", None),
            P(),
            P("head", None, None),
            P(("head", "tok"), None),
        ),
        out_specs=P("frame", ("head", "tok"), None),
        check_vma=False,
    )
```

```python
import functools

import jax
import jax.numpy as jnp
from jax import lax
from jax.experimental import pallas as pl
from jax.experimental.pallas import tpu as pltpu
from jax.sharding import PartitionSpec as P

MESH = pl.DeviceIdType.MESH
NX = 4
NY = 4
NZ = 4
OWN, LEFT, RIGHT, OPP = 0, 1, 2, 3


class Place:
    def __init__(self):
        self.frame = lax.axis_index("frame")
        self.head = lax.axis_index("head")
        self.core = lax.axis_index("tok")
        self.x, self.zh = self.head // NZ, self.head % NZ
        self.y, self.zl = self.frame // 2, self.frame % 2

    def to(self, x=0, z=0, y=0, frame=0, flip=False, core=None):
        head = ((self.x + x) % NX) * NZ + (self.zh + z) % NZ
        own = ((self.y + y) % NY) * 2 + self.zl if frame == 0 else self.frame + frame
        tok = self.core if core is None else core
        tok = 1 - tok if flip else tok
        return (own, head, tok)


class Copies:
    def __init__(self, send, recv):
        self.send, self.recv, self.count, self.all = send, recv, 0, {}

    def make(self, name, src, dst, device):
        k = self.count
        self.count += 1
        copy = pltpu.make_async_remote_copy(
            src_ref=src,
            dst_ref=dst,
            send_sem=self.send.at[k],
            recv_sem=self.recv.at[k],
            device_id=device,
            device_id_type=MESH,
        )
        self.all[name] = copy
        return copy

    def start(self, name, src, dst, device):
        self.make(name, src, dst, device).start()

    def got(self, *names):
        for name in names:
            self.all[name].wait_recv()

    def sent(self, skip=()):
        for name, copy in self.all.items():
            if name not in skip:
                copy.wait_send()


def greet(devices, count):
    barrier = pltpu.get_barrier_semaphore()
    for device in devices:
        pl.semaphore_signal(barrier, inc=1, device_id=device, device_id_type=MESH)
    pl.semaphore_wait(barrier, count)


class Gather:
    def __init__(self, tag, copies, me, ring, source, held, half, whole):
        self.tag, self.copies, self.me, self.ring = tag, copies, me, ring
        self.source, self.held, self.half, self.whole = source, held, half, whole
        self.mine = me.core * NY + me.y
        self.left = me.core * NY + (me.y + NY - 1) % NY
        self.right = me.core * NY + (me.y + 1) % NY
        self.far = me.core * NY + (me.y + 2) % NY

    def part(self, rel, eighth, which):
        return self.half(self.held, rel, eighth, which)

    def go(self, name, src, dst, device):
        self.copies.start(self.tag + name, src, dst, device)

    def got(self, *names):
        self.copies.got(*[self.tag + name for name in names])

    def ring_start(self):
        e = self.mine
        self.go("r", self.source(e), self.whole(self.held, LEFT, e), self.me.to(**{self.ring: 1}))
        self.go("l", self.source(e), self.whole(self.held, RIGHT, e), self.me.to(**{self.ring: -1}))

    def ring_relay(self):
        e = self.mine
        self.got("r")
        self.go("rr", self.part(LEFT, e, 0), self.part(OPP, e, 0), self.me.to(**{self.ring: 1}))
        self.y_start(LEFT)
        self.got("l")
        self.go("ll", self.part(RIGHT, e, 1), self.part(OPP, e, 1), self.me.to(**{self.ring: -1}))
        self.y_start(RIGHT)

    def ring_end(self):
        self.got("rr", "ll")
        self.y_start(OPP)

    def y_start(self, rel):
        n, e = str(rel), self.mine
        self.go("yr" + n, self.whole(self.held, rel, e), self.whole(self.held, rel, e), self.me.to(y=1))
        self.go("yl" + n, self.whole(self.held, rel, e), self.whole(self.held, rel, e), self.me.to(y=-1))
        self.go("s0" + n, self.whole(self.held, rel, e), self.whole(self.held, rel, e), self.me.to(flip=True))

    def y_relay(self, rel):
        n = str(rel)
        self.got("yr" + n)
        e = self.left
        self.go("yrr" + n, self.part(rel, e, 0), self.part(rel, e, 0), self.me.to(y=1))
        self.go("s1" + n, self.whole(self.held, rel, e), self.whole(self.held, rel, e), self.me.to(flip=True))
        self.got("yl" + n)
        e = self.right
        self.go("yll" + n, self.part(rel, e, 1), self.part(rel, e, 1), self.me.to(y=-1))
        self.go("s2" + n, self.whole(self.held, rel, e), self.whole(self.held, rel, e), self.me.to(flip=True))

    def y_end(self, rel):
        n = str(rel)
        self.got("yrr" + n, "yll" + n)
        e = self.far
        self.go("s3" + n, self.whole(self.held, rel, e), self.whole(self.held, rel, e), self.me.to(flip=True))

    def done(self, rel):
        n = str(rel)
        self.got("s0" + n, "s1" + n, "s2" + n, "s3" + n)


def rms_scale(values, gain):
    return values * lax.rsqrt(jnp.mean(values * values, axis=-1, keepdims=True) + 1e-06) * gain


def block_kernel(
    mods_ref, queue_ref, noise_ref, gains_ref, w_hbm, wo_hbm, out_ref,
    xg, wg, sb, rb, kvb, kt, vx, oa, top, attn_s, attn_g, wo, po, pr_s, pl_s, rl, rr, fl, fr,
    qb, ob, ou, local, send, recv,
):
    me = Place()
    core, frame = me.core, me.frame
    frames = lax.axis_size("frame")
    rows, width = queue_ref.shape[1:]
    hs = gains_ref.shape[1]
    bf16, f32 = jnp.bfloat16, jnp.float32
    half = width // 2
    tokens = NZ * rows
    keys = NX * 2 * tokens
    beside = frame + 2 * core - 1
    has_beside = jnp.logical_and(beside >= 0, beside < frames)
    after = (frame + 1) % frames
    before = (frame + frames - 1) % frames
    back = {LEFT: RIGHT, RIGHT: LEFT, OPP: OPP}
    shift = {LEFT: -1, RIGHT: 1, OPP: 2}

    own_w = pltpu.make_async_copy(w_hbm, wg.at[OWN], local.at[0])
    own_w.start()
    own_wo = pltpu.make_async_copy(wo_hbm, wo.at[OWN], local.at[1])
    own_wo.start()

    partners = [me.to(flip=True)]
    for step in (1, -1, 2):
        partners += [me.to(x=step), me.to(x=step, flip=True), me.to(z=step)]
    partners += [me.to(y=1), me.to(y=-1)]
    partners += [(before, me.head, 1)]
    barrier = pltpu.get_barrier_semaphore()
    for device in partners:
        pl.semaphore_signal(barrier, inc=1, device_id=device, device_id_type=MESH)

    @pl.when(core == 1)
    def _():
        for tok in range(2):
            pl.semaphore_signal(
                barrier, inc=1, device_id=(after, me.head, tok), device_id_type=MESH
            )

    pl.semaphore_wait(barrier, len(partners) + 2 * core)

    copies = Copies(send, recv)
    mine = me.core * NY + me.y
    seg = wg.shape[2]
    direct = seg // 4 // 32 * 32
    part = (seg - direct) // 2
    weights = Gather(
        "w", copies, me, "x", (lambda e: w_hbm.at[e, pl.ds(direct, 2 * part)]), wg,
        lambda ref, rel, e, which: ref.at[rel, e, pl.ds(direct + which * part, part)],
        lambda ref, rel, e: ref.at[rel, e, pl.ds(direct, 2 * part)],
    )
    weights.ring_start()
    quad = pl.ds(core * NY, NY)

    def rows_of(rel, first, count):
        return wg.at[rel, quad, pl.ds(first, count)]

    source = w_hbm.at[quad, pl.ds(0, direct)]
    copies.start("dr", source, rows_of(LEFT, 0, direct), me.to(x=1))
    copies.start("dl", source, rows_of(RIGHT, 0, direct), me.to(x=-1))

    for slot in range(2):
        x = queue_ref[slot].astype(f32)
        centred = x - jnp.mean(x, axis=-1, keepdims=True)
        normed = centred * lax.rsqrt(jnp.mean(centred * centred, axis=-1, keepdims=True) + 1e-06)
        xg[OWN, slot * rows : (slot + 1) * rows, :] = (
            normed * (1.0 + mods_ref[slot, 1:2, :]) + mods_ref[slot, 0:1, :]
        ).astype(bf16)
    first, second = pl.ds(0, rows), pl.ds(rows, rows)
    copies.start("zr0", xg.at[OWN, first], xg.at[LEFT, first], me.to(z=1))
    copies.start("zl1", xg.at[OWN, second], xg.at[RIGHT, second], me.to(z=-1))
    copies.start("zr1", xg.at[OWN, second], xg.at[LEFT, second], me.to(z=1))
    copies.start("zl0", xg.at[OWN, first], xg.at[RIGHT, first], me.to(z=-1))
    copies.start("qs", queue_ref.at[1 - core], qb.at[core], me.to(flip=True))

    weights.ring_relay()
    weights.ring_end()
    copies.got("zr0")
    copies.start("zrr", xg.at[LEFT, first], xg.at[OPP, first], me.to(z=1))
    copies.got("zl1")
    copies.start("zll", xg.at[RIGHT, second], xg.at[OPP, second], me.to(z=-1))
    copies.got("dr")
    low, high = direct // 2, direct - direct // 2
    copies.start("drr", rows_of(LEFT, 0, low), rows_of(OPP, 0, low), me.to(x=1))
    copies.start("ds1", rows_of(LEFT, 0, direct), rows_of(LEFT, 0, direct), me.to(flip=True))
    copies.got("dl")
    copies.start("dll", rows_of(RIGHT, low, high), rows_of(OPP, low, high), me.to(x=-1))
    copies.start("ds2", rows_of(RIGHT, 0, direct), rows_of(RIGHT, 0, direct), me.to(flip=True))
    weights.y_relay(LEFT)
    weights.y_relay(RIGHT)
    weights.y_end(LEFT)
    copies.got("drr", "dll")
    copies.start("ds3", rows_of(OPP, 0, direct), rows_of(OPP, 0, direct), me.to(flip=True))

    q_gain = gains_ref[0:1, :] * f32(1.4426950408889634 / hs**0.5)
    k_gain = gains_ref[1:2, :]
    groups = (pl.ds(0, NZ - 1), pl.ds(NZ - 1, 1))
    sizes = (NZ - 1, 1)

    def project(rel, group):
        which, count = groups[group], sizes[group]
        xs = xg[which].reshape(count * 2 * rows, width)
        w = wg[rel].reshape(width, 3 * hs)
        qkv = jnp.dot(xs, w, preferred_element_type=f32)
        q = rms_scale(qkv[:, :hs], q_gain)
        k = rms_scale(qkv[:, hs : 2 * hs], k_gain)
        out = jnp.concatenate([q, k, qkv[:, 2 * hs :]], axis=-1).astype(bf16)
        out = out.reshape(count, 2, rows, 3 * hs)
        for slot in range(2):
            sb[rel, slot, which] = out[:, slot]
        n = f"{rel}{group}"
        if rel == OWN:
            copies.start(
                "a" + n, sb.at[OWN, 1 - core, which], rb.at[core, which], me.to(flip=True)
            )
            rb[core, which] = sb[OWN, core, which]
            return
        spot = rb.at[back[rel] * 2 + core, which]
        copies.start("a" + n, sb.at[rel, core, which], spot, me.to(x=shift[rel]))
        copies.start("b" + n, sb.at[rel, 1 - core, which], spot, me.to(x=shift[rel], flip=True))

    def share(rel, group):
        n = f"{rel}{group}"
        copies.got("a" + n)
        if rel != OWN:
            copies.got("b" + n)
        spot = OWN if rel == OWN else back[rel]
        pair = pl.ds(spot * 2, 2)
        src = rb.at[pair, groups[group], :, pl.ds(hs, 2 * hs)]
        dst = kvb.at[1, pair, groups[group]]
        side = copies.make("kv" + n, src, dst, (beside, me.head, 1 - core))

        @pl.when(has_beside)
        def _():
            side.start()

        copies.start("ks" + n, src, kvb.at[0, pair, groups[group]], me.to(flip=True))

    own_w.wait()
    copies.got("zr1", "zl0")
    project(OWN, 0)
    weights.y_relay(OPP)
    weights.done(LEFT)
    copies.got("ds1")
    project(LEFT, 0)
    weights.y_end(RIGHT)
    weights.done(RIGHT)
    copies.got("ds2")
    project(RIGHT, 0)
    share(OWN, 0)
    copies.got("zrr", "zll")
    project(OWN, 1)
    project(LEFT, 1)
    project(RIGHT, 1)
    weights.y_end(OPP)
    weights.done(OPP)
    copies.got("ds3")
    project(OPP, 0)
    project(OPP, 1)
    outs = Gather(
        "o", copies, me, "z", (lambda e: wo_hbm.at[e]), wo,
        lambda ref, rel, e, which: ref.at[rel, e, :, pl.ds(which * half, half)],
        lambda ref, rel, e: ref.at[rel, e],
    )
    outs.ring_start()
    share(LEFT, 0)
    share(RIGHT, 0)
    share(OWN, 1)
    share(LEFT, 1)
    share(RIGHT, 1)
    share(OPP, 0)
    share(OPP, 1)
    names = [f"{rel}{group}" for rel in range(4) for group in range(2)]

    ones = jnp.ones((keys, hs), bf16)

    def take(which, kv):
        kt[which] = kv[:, :hs].T
        vx[which, :, :hs] = kv[:, hs:]
        vx[which, :, hs:] = ones

    take(0, rb[...].reshape(keys, 3 * hs)[:, hs:])
    outs.ring_relay()
    copies.got(*["ks" + n for n in names])
    take(1, kvb[0].reshape(keys, 2 * hs))
    outs.ring_end()

    block = tokens

    def queries(i):
        return rb[i].reshape(block, 3 * hs)[:, :hs]

    @pl.loop(0, 2 * NX)
    def _(i):
        q = queries(i)
        scores = [jnp.dot(q, kt[j], preferred_element_type=f32) for j in range(2)]
        peak = jnp.maximum(
            jnp.max(scores[0], axis=-1, keepdims=True), jnp.max(scores[1], axis=-1, keepdims=True)
        )
        total = jnp.zeros((block, 2 * hs), f32)
        for j in range(2):
            p = jnp.exp2(scores[j] - peak).astype(bf16)
            total += jnp.dot(p, vx[j], preferred_element_type=f32)
        oa[i] = total
        top[i] = jnp.broadcast_to(peak, (block, hs))

    for rel in (LEFT, RIGHT, OPP):
        outs.y_relay(rel)

    @pl.when(has_beside)
    def _():
        for n in names:
            copies.got("kv" + n)
        take(2, kvb[1].reshape(keys, 2 * hs))

    def attend(rx):
        @pl.when(has_beside)
        def _():
            @pl.loop(2 * rx, 2 * rx + 2)
            def _(i):
                s = jnp.dot(queries(i), kt[2], preferred_element_type=f32)
                old = top[i][:, :1]
                peak = jnp.maximum(old, jnp.max(s, axis=-1, keepdims=True))
                p = jnp.exp2(s - peak).astype(bf16)
                oa[i] = oa[i] * jnp.exp2(old - peak) + jnp.dot(
                    p, vx[2], preferred_element_type=f32
                )

        o = oa[2 * rx : 2 * rx + 2].reshape(2 * tokens, 2 * hs)
        attn = (o[:, :hs] / o[:, hs:]).astype(bf16).reshape(2, NZ, rows, hs)
        attn_g[rx, OWN] = attn[:, OWN].reshape(2 * rows, hs)
        for rz in (LEFT, RIGHT, OPP):
            attn_s[rx, rz] = attn[:, rz].reshape(2 * rows, hs)
            copies.start(
                f"t{rx}{rz}", attn_s.at[rx, rz], attn_g.at[rx, back[rz]], me.to(z=shift[rz])
            )

    def contribution(rx):
        copies.got(*[f"t{rx}{rz}" for rz in (LEFT, RIGHT, OPP)])
        a = jnp.concatenate([attn_g[rx, rz] for rz in range(NZ)], axis=-1)
        return jnp.dot(a, wo[...].reshape(NZ * hs, width), preferred_element_type=f32)

    attend(OPP)
    for rel in (LEFT, RIGHT, OPP):
        outs.y_end(rel)
    attend(RIGHT)
    attend(LEFT)
    own_wo.wait()
    for rel in (LEFT, RIGHT, OPP):
        outs.done(rel)

    sub = half // 2
    p = contribution(OPP).astype(bf16)
    for j in range(2):
        po[j] = p[:, j * sub : (j + 1) * sub]
        po[2 + j] = p[:, half + j * sub : half + (j + 1) * sub]
        copies.start(f"rl{j}", po.at[j], rl.at[j], me.to(x=1))
        copies.start(f"rr{j}", po.at[2 + j], rr.at[j], me.to(x=-1))
    attend(OWN)

    right = contribution(RIGHT)
    for j in range(2):
        pr_s[2 + j] = right[:, half + j * sub : half + (j + 1) * sub].astype(bf16)
        copies.start(f"fl{2 + j}", pr_s.at[2 + j], fl.at[2 + j], me.to(x=1))
    left = contribution(LEFT)
    for j in range(2):
        pl_s[j] = left[:, j * sub : (j + 1) * sub].astype(bf16)
        copies.start(f"fr{j}", pl_s.at[j], fr.at[j], me.to(x=-1))
    for j in range(2):
        copies.got(f"rl{j}")
        pr_s[j] = (right[:, j * sub : (j + 1) * sub] + rl[j].astype(f32)).astype(bf16)
        copies.start(f"fl{j}", pr_s.at[j], fl.at[j], me.to(x=1))
        copies.got(f"rr{j}")
        pl_s[2 + j] = (
            left[:, half + j * sub : half + (j + 1) * sub] + rr[j].astype(f32)
        ).astype(bf16)
        copies.start(f"fr{2 + j}", pl_s.at[2 + j], fr.at[2 + j], me.to(x=-1))

    p = contribution(OWN)
    copies.got("qs")
    qb[core] = queue_ref[core]
    gate = mods_ref[core, 2:3, :]
    sends_on = jnp.logical_and(core == 1, frame < frames - 1)
    near, next0, next1 = {}, {}, {}
    for j in range(2):
        copies.got(f"fl{j}", f"fr{j}", f"fl{2 + j}", f"fr{2 + j}")
        for h in (j, 2 + j):
            cols = slice(h * sub, (h + 1) * sub)
            proj = p[:, cols] + fl[h].astype(f32) + fr[h].astype(f32)
            for tok in range(2):
                ob[h, tok] = (
                    qb[tok, :, cols].astype(f32)
                    + gate[:, cols] * proj[tok * rows : (tok + 1) * rows]
                ).astype(bf16)
        for h in (j, 2 + j):
            near[h] = copies.make(f"o{h}", ob.at[h, 1], ou.at[1, h], me.to(flip=True))
            next0[h] = copies.make(f"n{h}", ob.at[h, 0], ou.at[0, h], (after, me.head, 0))
            next1[h] = pltpu.make_async_remote_copy(
                src_ref=ob.at[h, 1], dst_ref=ou.at[0, h],
                send_sem=local.at[2 + h], recv_sem=recv.at[copies.count - 1],
                device_id=(after, me.head, 1), device_id_type=MESH,
            )

        @pl.when(core == 0)
        def _():
            for h in (j, 2 + j):
                near[h].start()
                out_ref[1, :, h * sub : (h + 1) * sub] = ob[h, 0]

        @pl.when(sends_on)
        def _():
            for h in (j, 2 + j):
                next0[h].start()
                next1[h].start()

    @pl.when(frame == 0)
    def _():
        out_ref[0] = noise_ref[...]

    @pl.when(core == 1)
    def _():
        for h in range(4):
            near[h].wait_recv()
            out_ref[1, :, h * sub : (h + 1) * sub] = ou[1, h]

    @pl.when(frame > 0)
    def _():
        for h in range(4):
            next0[h].wait_recv()
            out_ref[0, :, h * sub : (h + 1) * sub] = ou[0, h]

    @pl.when(core == 0)
    def _():
        for h in range(4):
            near[h].wait_send()

    @pl.when(sends_on)
    def _():
        for h in range(4):
            next0[h].wait_send()
            next1[h].wait_send()

    @pl.when(has_beside)
    def _():
        for n in names:
            copies.all["kv" + n].wait_send()

    copies.sent(skip=[f"{t}{h}" for t in "on" for h in range(4)] + ["kv" + n for n in names])


def body(queue, timesteps, mod_table, w_qkv, norm_gains, w_out, noise_frame):
    slots, rows, width = queue.shape
    hs = w_out.shape[1]
    bf16, f32 = jnp.bfloat16, jnp.float32
    vmem = pl.BlockSpec(memory_space=pltpu.VMEM)
    hbm = pl.BlockSpec(memory_space=pl.ANY)
    tokens = NZ * rows
    keys = NX * 2 * tokens
    eighth = width // 8
    half = width // 2
    sub = half // 2
    mods = jnp.stack(
        [lax.dynamic_index_in_dim(mod_table, timesteps[i], 0, keepdims=False) for i in range(slots)]
    )
    return pl.pallas_call(
        block_kernel,
        out_shape=jax.ShapeDtypeStruct(queue.shape, bf16),
        in_specs=[vmem, vmem, vmem, vmem, hbm, hbm],
        out_specs=vmem,
        scratch_shapes=[
            pltpu.VMEM((NZ, 2 * rows, width), bf16),
            pltpu.VMEM((NX, 8, eighth, 3 * hs), bf16),
            pltpu.VMEM((NX, 2, NZ, rows, 3 * hs), bf16),
            pltpu.VMEM((NX * 2, NZ, rows, 3 * hs), bf16),
            pltpu.VMEM((2, NX * 2, NZ, rows, 2 * hs), bf16),
            pltpu.VMEM((3, hs, keys), bf16),
            pltpu.VMEM((3, keys, 2 * hs), bf16),
            pltpu.VMEM((NX * 2, tokens, 2 * hs), f32),
            pltpu.VMEM((NX * 2, tokens, hs), f32),
            pltpu.VMEM((NX, NZ, 2 * rows, hs), bf16),
            pltpu.VMEM((NX, NZ, 2 * rows, hs), bf16),
            pltpu.VMEM((NZ, 8, hs // 8, width), bf16),
            pltpu.VMEM((4, 2 * rows, sub), bf16),
            pltpu.VMEM((4, 2 * rows, sub), bf16),
            pltpu.VMEM((4, 2 * rows, sub), bf16),
            pltpu.VMEM((2, 2 * rows, sub), bf16),
            pltpu.VMEM((2, 2 * rows, sub), bf16),
            pltpu.VMEM((4, 2 * rows, sub), bf16),
            pltpu.VMEM((4, 2 * rows, sub), bf16),
            pltpu.VMEM((2, rows, width), bf16),
            pltpu.VMEM((4, 2, rows, sub), bf16),
            pltpu.VMEM((2, 4, rows, sub), bf16),
            pltpu.SemaphoreType.DMA((6,)),
            pltpu.SemaphoreType.DMA((160,)),
            pltpu.SemaphoreType.DMA((160,)),
        ],
        compiler_params=pltpu.CompilerParams(
            collective_id=0, has_side_effects=True, vmem_limit_bytes=56 * 1024 * 1024
        ),
        name="block",
    )(
        mods, queue, noise_frame, norm_gains,
        w_qkv.reshape(8, eighth, 3 * hs), w_out.reshape(8, hs // 8, width),
    )


def solution(mesh):
    return jax.shard_map(
        body,
        mesh=mesh,
        in_specs=(
            P("frame", ("head", "tok"), None),
            P("frame"),
            P(),
            P(None, "head", None),
            P(),
            P("head", None, None),
            P(("head", "tok"), None),
        ),
        out_specs=P("frame", ("head", "tok"), None),
        check_vma=False,
    )
```

```python
import functools

import jax
import jax.numpy as jnp
from jax import lax
from jax.experimental import pallas as pl
from jax.experimental.pallas import tpu as pltpu
from jax.sharding import PartitionSpec as P

MESH = pl.DeviceIdType.MESH
NX = 4
NY = 4
NZ = 4
OWN, LEFT, RIGHT, OPP = 0, 1, 2, 3


class Place:
    def __init__(self):
        self.frame = lax.axis_index("frame")
        self.head = lax.axis_index("head")
        self.core = lax.axis_index("tok")
        self.x, self.zh = self.head // NZ, self.head % NZ
        self.y, self.zl = self.frame // 2, self.frame % 2

    def to(self, x=0, z=0, y=0, frame=0, flip=False, core=None):
        head = ((self.x + x) % NX) * NZ + (self.zh + z) % NZ
        own = ((self.y + y) % NY) * 2 + self.zl if frame == 0 else self.frame + frame
        tok = self.core if core is None else core
        tok = 1 - tok if flip else tok
        return (own, head, tok)


class Copies:
    def __init__(self, send, recv):
        self.send, self.recv, self.count, self.all = send, recv, 0, {}

    def make(self, name, src, dst, device):
        k = self.count
        self.count += 1
        copy = pltpu.make_async_remote_copy(
            src_ref=src,
            dst_ref=dst,
            send_sem=self.send.at[k],
            recv_sem=self.recv.at[k],
            device_id=device,
            device_id_type=MESH,
        )
        self.all[name] = copy
        return copy

    def start(self, name, src, dst, device):
        self.make(name, src, dst, device).start()

    def got(self, *names):
        for name in names:
            self.all[name].wait_recv()

    def sent(self, skip=()):
        for name, copy in self.all.items():
            if name not in skip:
                copy.wait_send()


def greet(devices, count):
    barrier = pltpu.get_barrier_semaphore()
    for device in devices:
        pl.semaphore_signal(barrier, inc=1, device_id=device, device_id_type=MESH)
    pl.semaphore_wait(barrier, count)


class Gather:
    def __init__(self, tag, copies, me, ring, source, held, half, whole):
        self.tag, self.copies, self.me, self.ring = tag, copies, me, ring
        self.source, self.held, self.half, self.whole = source, held, half, whole
        self.mine = me.core * NY + me.y
        self.left = me.core * NY + (me.y + NY - 1) % NY
        self.right = me.core * NY + (me.y + 1) % NY
        self.far = me.core * NY + (me.y + 2) % NY

    def part(self, rel, eighth, which):
        return self.half(self.held, rel, eighth, which)

    def go(self, name, src, dst, device):
        self.copies.start(self.tag + name, src, dst, device)

    def got(self, *names):
        self.copies.got(*[self.tag + name for name in names])

    def ring_start(self):
        e = self.mine
        self.go("r", self.source(e), self.whole(self.held, LEFT, e), self.me.to(**{self.ring: 1}))
        self.go("l", self.source(e), self.whole(self.held, RIGHT, e), self.me.to(**{self.ring: -1}))

    def ring_relay(self):
        e = self.mine
        self.got("r")
        self.go("rr", self.part(LEFT, e, 0), self.part(OPP, e, 0), self.me.to(**{self.ring: 1}))
        self.y_start(LEFT)
        self.got("l")
        self.go("ll", self.part(RIGHT, e, 1), self.part(OPP, e, 1), self.me.to(**{self.ring: -1}))
        self.y_start(RIGHT)

    def ring_end(self):
        self.got("rr", "ll")
        self.y_start(OPP)

    def y_start(self, rel):
        n, e = str(rel), self.mine
        self.go("yr" + n, self.whole(self.held, rel, e), self.whole(self.held, rel, e), self.me.to(y=1))
        self.go("yl" + n, self.whole(self.held, rel, e), self.whole(self.held, rel, e), self.me.to(y=-1))
        self.go("s0" + n, self.whole(self.held, rel, e), self.whole(self.held, rel, e), self.me.to(flip=True))

    def y_relay(self, rel):
        n = str(rel)
        self.got("yr" + n)
        e = self.left
        self.go("yrr" + n, self.part(rel, e, 0), self.part(rel, e, 0), self.me.to(y=1))
        self.go("s1" + n, self.whole(self.held, rel, e), self.whole(self.held, rel, e), self.me.to(flip=True))
        self.got("yl" + n)
        e = self.right
        self.go("yll" + n, self.part(rel, e, 1), self.part(rel, e, 1), self.me.to(y=-1))
        self.go("s2" + n, self.whole(self.held, rel, e), self.whole(self.held, rel, e), self.me.to(flip=True))

    def y_end(self, rel):
        n = str(rel)
        self.got("yrr" + n, "yll" + n)
        e = self.far
        self.go("s3" + n, self.whole(self.held, rel, e), self.whole(self.held, rel, e), self.me.to(flip=True))

    def done(self, rel):
        n = str(rel)
        self.got("s0" + n, "s1" + n, "s2" + n, "s3" + n)


def rms_scale(values, gain):
    return values * lax.rsqrt(jnp.mean(values * values, axis=-1, keepdims=True) + 1e-06) * gain


def block_kernel(
    steps_ref, mod_hbm, queue_ref, noise_ref, gains_ref, w_hbm, wo_hbm, out_ref,
    mod, xg, wg, sb, rb, kvb, kt, vx, oa, top, attn_s, attn_g, wo, po, pr_s, pl_s, rl, rr, fl, fr,
    qb, ob, ou, local, send, recv,
):
    me = Place()
    core, frame = me.core, me.frame
    frames = lax.axis_size("frame")
    rows, width = queue_ref.shape[1:]
    hs = gains_ref.shape[1]
    bf16, f32 = jnp.bfloat16, jnp.float32
    half = width // 2
    tokens = NZ * rows
    keys = NX * 2 * tokens
    beside = frame + 2 * core - 1
    has_beside = jnp.logical_and(beside >= 0, beside < frames)
    after = (frame + 1) % frames
    before = (frame + frames - 1) % frames
    back = {LEFT: RIGHT, RIGHT: LEFT, OPP: OPP}
    shift = {LEFT: -1, RIGHT: 1, OPP: 2}

    mod_copy = pltpu.make_async_copy(mod_hbm, mod, local.at[6])
    mod_copy.start()
    own_w = pltpu.make_async_copy(w_hbm, wg.at[OWN], local.at[0])
    own_w.start()
    own_wo = pltpu.make_async_copy(wo_hbm, wo.at[OWN], local.at[1])
    own_wo.start()

    partners = [me.to(flip=True)]
    for step in (1, -1, 2):
        partners += [me.to(x=step), me.to(x=step, flip=True), me.to(z=step)]
    partners += [me.to(y=1), me.to(y=-1)]
    partners += [(before, me.head, 1)]
    barrier = pltpu.get_barrier_semaphore()
    for device in partners:
        pl.semaphore_signal(barrier, inc=1, device_id=device, device_id_type=MESH)

    @pl.when(core == 1)
    def _():
        for tok in range(2):
            pl.semaphore_signal(
                barrier, inc=1, device_id=(after, me.head, tok), device_id_type=MESH
            )

    mod_copy.wait()
    for slot in range(2):
        level = pl.ds(steps_ref[slot], 1)
        x = queue_ref[slot].astype(f32)
        centred = x - jnp.mean(x, axis=-1, keepdims=True)
        normed = centred * lax.rsqrt(jnp.mean(centred * centred, axis=-1, keepdims=True) + 1e-06)
        xg[OWN, slot * rows : (slot + 1) * rows, :] = (
            normed * (1.0 + mod[1, level, :]) + mod[0, level, :]
        ).astype(bf16)

    pl.semaphore_wait(barrier, len(partners) + 2 * core)

    copies = Copies(send, recv)
    mine = me.core * NY + me.y
    seg = wg.shape[2]
    direct = seg // 3 // 32 * 32
    part = (seg - direct) // 2
    weights = Gather(
        "w", copies, me, "x", (lambda e: w_hbm.at[e, pl.ds(direct, 2 * part)]), wg,
        lambda ref, rel, e, which: ref.at[rel, e, pl.ds(direct + which * part, part)],
        lambda ref, rel, e: ref.at[rel, e, pl.ds(direct, 2 * part)],
    )
    weights.ring_start()
    quad = pl.ds(core * NY, NY)

    def rows_of(rel, first, count):
        return wg.at[rel, quad, pl.ds(first, count)]

    first, second = pl.ds(0, rows), pl.ds(rows, rows)
    copies.start("zr0", xg.at[OWN, first], xg.at[LEFT, first], me.to(z=1))
    copies.start("zl1", xg.at[OWN, second], xg.at[RIGHT, second], me.to(z=-1))
    copies.start("zr1", xg.at[OWN, second], xg.at[LEFT, second], me.to(z=1))
    copies.start("zl0", xg.at[OWN, first], xg.at[RIGHT, first], me.to(z=-1))
    copies.start("qs", queue_ref.at[1 - core], qb.at[core], me.to(flip=True))

    weights.ring_relay()
    source = w_hbm.at[quad, pl.ds(0, direct)]
    copies.start("dr", source, rows_of(LEFT, 0, direct), me.to(x=1))
    copies.start("dl", source, rows_of(RIGHT, 0, direct), me.to(x=-1))
    copies.got("zr0")
    copies.start("zrr", xg.at[LEFT, first], xg.at[OPP, first], me.to(z=1))
    copies.got("zl1")
    copies.start("zll", xg.at[RIGHT, second], xg.at[OPP, second], me.to(z=-1))
    outs = Gather(
        "o", copies, me, "z", (lambda e: wo_hbm.at[e]), wo,
        lambda ref, rel, e, which: ref.at[rel, e, :, pl.ds(which * half, half)],
        lambda ref, rel, e: ref.at[rel, e],
    )
    outs.ring_start()
    weights.ring_end()
    weights.y_relay(LEFT)
    copies.got("dr")
    low, high = direct // 2, direct - direct // 2
    copies.start("drr", rows_of(LEFT, 0, low), rows_of(OPP, 0, low), me.to(x=1))
    copies.start("ds1", rows_of(LEFT, 0, direct), rows_of(LEFT, 0, direct), me.to(flip=True))
    copies.got("dl")
    copies.start("dll", rows_of(RIGHT, low, high), rows_of(OPP, low, high), me.to(x=-1))
    copies.start("ds2", rows_of(RIGHT, 0, direct), rows_of(RIGHT, 0, direct), me.to(flip=True))
    weights.y_relay(RIGHT)

    q_gain = gains_ref[0:1, :] * f32(1.4426950408889634 / hs**0.5)
    k_gain = gains_ref[1:2, :]
    groups = (pl.ds(0, NZ - 1), pl.ds(NZ - 1, 1))
    sizes = (NZ - 1, 1)

    def project(rel, group):
        which, count = groups[group], sizes[group]
        xs = xg[which].reshape(count * 2 * rows, width)
        w = wg[rel].reshape(width, 3 * hs)
        qkv = jnp.dot(xs, w, preferred_element_type=f32)
        q = rms_scale(qkv[:, :hs], q_gain)
        k = rms_scale(qkv[:, hs : 2 * hs], k_gain)
        out = jnp.concatenate([q, k, qkv[:, 2 * hs :]], axis=-1).astype(bf16)
        out = out.reshape(count, 2, rows, 3 * hs)
        for slot in range(2):
            sb[rel, slot, which] = out[:, slot]
        n = f"{rel}{group}"
        if rel == OWN:
            copies.start(
                "a" + n, sb.at[OWN, 1 - core, which], rb.at[core, which], me.to(flip=True)
            )
            rb[core, which] = sb[OWN, core, which]
            return
        spot = rb.at[back[rel] * 2 + core, which]
        copies.start("a" + n, sb.at[rel, core, which], spot, me.to(x=shift[rel]))
        copies.start("b" + n, sb.at[rel, 1 - core, which], spot, me.to(x=shift[rel], flip=True))

    def share(rel, group):
        n = f"{rel}{group}"
        copies.got("a" + n)
        if rel != OWN:
            copies.got("b" + n)
        spot = OWN if rel == OWN else back[rel]
        pair = pl.ds(spot * 2, 2)
        src = rb.at[pair, groups[group], :, pl.ds(hs, 2 * hs)]
        dst = kvb.at[1, pair, groups[group]]
        side = copies.make("kv" + n, src, dst, (beside, me.head, 1 - core))

        @pl.when(has_beside)
        def _():
            side.start()

        copies.start("ks" + n, src, kvb.at[0, pair, groups[group]], me.to(flip=True))

    own_w.wait()
    copies.got("zr1", "zl0")
    project(OWN, 0)
    weights.y_relay(OPP)
    weights.y_end(LEFT)
    weights.done(LEFT)
    copies.got("ds1")
    project(LEFT, 0)
    share(OWN, 0)
    weights.y_end(RIGHT)
    weights.done(RIGHT)
    copies.got("ds2")
    project(RIGHT, 0)
    copies.got("drr", "dll")
    copies.start("ds3", rows_of(OPP, 0, direct), rows_of(OPP, 0, direct), me.to(flip=True))
    share(LEFT, 0)
    weights.y_end(OPP)
    copies.got("zrr", "zll")
    project(OWN, 1)
    project(LEFT, 1)
    project(RIGHT, 1)
    share(RIGHT, 0)
    weights.done(OPP)
    copies.got("ds3")
    project(OPP, 0)
    project(OPP, 1)
    share(OWN, 1)
    share(LEFT, 1)
    share(RIGHT, 1)
    outs.ring_relay()
    share(OPP, 0)
    share(OPP, 1)
    names = [f"{rel}{group}" for rel in range(4) for group in range(2)]

    ones = jnp.ones((keys, hs), bf16)

    def take(which, kv):
        kt[which] = kv[:, :hs].T
        vx[which, :, :hs] = kv[:, hs:]
        vx[which, :, hs:] = ones

    take(0, rb[...].reshape(keys, 3 * hs)[:, hs:])
    outs.ring_end()
    copies.got(*["ks" + n for n in names])
    take(1, kvb[0].reshape(keys, 2 * hs))

    block = 2 * tokens

    def queries(i):
        return rb[pl.ds(2 * i, 2)].reshape(block, 3 * hs)[:, :hs]

    @pl.loop(0, NX)
    def _(i):
        q = queries(i)
        scores = [jnp.dot(q, kt[j], preferred_element_type=f32) for j in range(2)]
        peak = jnp.maximum(
            jnp.max(scores[0], axis=-1, keepdims=True), jnp.max(scores[1], axis=-1, keepdims=True)
        )
        total = jnp.zeros((block, 2 * hs), f32)
        for j in range(2):
            p = jnp.exp2(scores[j] - peak).astype(bf16)
            total += jnp.dot(p, vx[j], preferred_element_type=f32)
        oa[i] = total
        top[i] = jnp.broadcast_to(peak, (block, hs))

    for rel in (LEFT, RIGHT, OPP):
        outs.y_relay(rel)

    @pl.when(has_beside)
    def _():
        for n in names:
            copies.got("kv" + n)
        take(2, kvb[1].reshape(keys, 2 * hs))

    def attend(rx):
        @pl.when(has_beside)
        def _():
            s = jnp.dot(queries(rx), kt[2], preferred_element_type=f32)
            old = top[rx][:, :1]
            peak = jnp.maximum(old, jnp.max(s, axis=-1, keepdims=True))
            p = jnp.exp2(s - peak).astype(bf16)
            oa[rx] = oa[rx] * jnp.exp2(old - peak) + jnp.dot(
                p, vx[2], preferred_element_type=f32
            )

        o = oa[rx]
        attn = (o[:, :hs] / o[:, hs:]).astype(bf16).reshape(2, NZ, rows, hs)
        attn_g[rx, OWN] = attn[:, OWN].reshape(2 * rows, hs)
        for rz in (LEFT, RIGHT, OPP):
            attn_s[rx, rz] = attn[:, rz].reshape(2 * rows, hs)
            copies.start(
                f"t{rx}{rz}", attn_s.at[rx, rz], attn_g.at[rx, back[rz]], me.to(z=shift[rz])
            )

    def contribution(rx):
        copies.got(*[f"t{rx}{rz}" for rz in (LEFT, RIGHT, OPP)])
        a = jnp.concatenate([attn_g[rx, rz] for rz in range(NZ)], axis=-1)
        return jnp.dot(a, wo[...].reshape(NZ * hs, width), preferred_element_type=f32)

    attend(OPP)
    for rel in (LEFT, RIGHT, OPP):
        outs.y_end(rel)
    attend(RIGHT)
    attend(LEFT)
    own_wo.wait()
    for rel in (LEFT, RIGHT, OPP):
        outs.done(rel)

    sub = half // 2
    p = contribution(OPP).astype(bf16)
    for j in range(2):
        po[j] = p[:, j * sub : (j + 1) * sub]
        po[2 + j] = p[:, half + j * sub : half + (j + 1) * sub]
        copies.start(f"rl{j}", po.at[j], rl.at[j], me.to(x=1))
        copies.start(f"rr{j}", po.at[2 + j], rr.at[j], me.to(x=-1))
    attend(OWN)

    right = contribution(RIGHT)
    for j in range(2):
        pr_s[2 + j] = right[:, half + j * sub : half + (j + 1) * sub].astype(bf16)
        copies.start(f"fl{2 + j}", pr_s.at[2 + j], fl.at[2 + j], me.to(x=1))
    left = contribution(LEFT)
    for j in range(2):
        pl_s[j] = left[:, j * sub : (j + 1) * sub].astype(bf16)
        copies.start(f"fr{j}", pl_s.at[j], fr.at[j], me.to(x=-1))
    for j in range(2):
        copies.got(f"rl{j}")
        pr_s[j] = (right[:, j * sub : (j + 1) * sub] + rl[j].astype(f32)).astype(bf16)
        copies.start(f"fl{j}", pr_s.at[j], fl.at[j], me.to(x=1))
        copies.got(f"rr{j}")
        pl_s[2 + j] = (
            left[:, half + j * sub : half + (j + 1) * sub] + rr[j].astype(f32)
        ).astype(bf16)
        copies.start(f"fr{2 + j}", pl_s.at[2 + j], fr.at[2 + j], me.to(x=-1))

    p = contribution(OWN)
    copies.got("qs")
    qb[core] = queue_ref[core]
    gate = mod[2, pl.ds(steps_ref[core], 1), :]
    sends_on = jnp.logical_and(core == 1, frame < frames - 1)
    near, next0, next1 = {}, {}, {}
    for j in range(2):
        copies.got(f"fl{j}", f"fr{j}", f"fl{2 + j}", f"fr{2 + j}")
        for h in (j, 2 + j):
            cols = slice(h * sub, (h + 1) * sub)
            proj = p[:, cols] + fl[h].astype(f32) + fr[h].astype(f32)
            for tok in range(2):
                ob[h, tok] = (
                    qb[tok, :, cols].astype(f32)
                    + gate[:, cols] * proj[tok * rows : (tok + 1) * rows]
                ).astype(bf16)
        for h in (j, 2 + j):
            near[h] = copies.make(f"o{h}", ob.at[h, 1], ou.at[1, h], me.to(flip=True))
            next0[h] = copies.make(f"n{h}", ob.at[h, 0], ou.at[0, h], (after, me.head, 0))
            next1[h] = pltpu.make_async_remote_copy(
                src_ref=ob.at[h, 1], dst_ref=ou.at[0, h],
                send_sem=local.at[2 + h], recv_sem=recv.at[copies.count - 1],
                device_id=(after, me.head, 1), device_id_type=MESH,
            )

        @pl.when(core == 0)
        def _():
            for h in (j, 2 + j):
                near[h].start()
                out_ref[1, :, h * sub : (h + 1) * sub] = ob[h, 0]

        @pl.when(sends_on)
        def _():
            for h in (j, 2 + j):
                next0[h].start()
                next1[h].start()

    @pl.when(frame == 0)
    def _():
        out_ref[0] = noise_ref[...]

    @pl.when(core == 1)
    def _():
        for h in range(4):
            near[h].wait_recv()
            out_ref[1, :, h * sub : (h + 1) * sub] = ou[1, h]

    @pl.when(frame > 0)
    def _():
        for h in range(4):
            next0[h].wait_recv()
            out_ref[0, :, h * sub : (h + 1) * sub] = ou[0, h]

    @pl.when(core == 0)
    def _():
        for h in range(4):
            near[h].wait_send()

    @pl.when(sends_on)
    def _():
        for h in range(4):
            next0[h].wait_send()
            next1[h].wait_send()

    @pl.when(has_beside)
    def _():
        for n in names:
            copies.all["kv" + n].wait_send()

    copies.sent(skip=[f"{t}{h}" for t in "on" for h in range(4)] + ["kv" + n for n in names])


def body(queue, timesteps, mod_table, w_qkv, norm_gains, w_out, noise_frame):
    slots, rows, width = queue.shape
    hs = w_out.shape[1]
    bf16, f32 = jnp.bfloat16, jnp.float32
    vmem = pl.BlockSpec(memory_space=pltpu.VMEM)
    hbm = pl.BlockSpec(memory_space=pl.ANY)
    smem = pl.BlockSpec(memory_space=pltpu.SMEM)
    tokens = NZ * rows
    keys = NX * 2 * tokens
    eighth = width // 8
    half = width // 2
    sub = half // 2
    table = jnp.transpose(mod_table, (1, 0, 2))
    return pl.pallas_call(
        block_kernel,
        out_shape=jax.ShapeDtypeStruct(queue.shape, bf16),
        in_specs=[smem, hbm, vmem, vmem, vmem, hbm, hbm],
        out_specs=vmem,
        scratch_shapes=[
            pltpu.VMEM(table.shape, f32),
            pltpu.VMEM((NZ, 2 * rows, width), bf16),
            pltpu.VMEM((NX, 8, eighth, 3 * hs), bf16),
            pltpu.VMEM((NX, 2, NZ, rows, 3 * hs), bf16),
            pltpu.VMEM((NX * 2, NZ, rows, 3 * hs), bf16),
            pltpu.VMEM((2, NX * 2, NZ, rows, 2 * hs), bf16),
            pltpu.VMEM((3, hs, keys), bf16),
            pltpu.VMEM((3, keys, 2 * hs), bf16),
            pltpu.VMEM((NX, 2 * tokens, 2 * hs), f32),
            pltpu.VMEM((NX, 2 * tokens, hs), f32),
            pltpu.VMEM((NX, NZ, 2 * rows, hs), bf16),
            pltpu.VMEM((NX, NZ, 2 * rows, hs), bf16),
            pltpu.VMEM((NZ, 8, hs // 8, width), bf16),
            pltpu.VMEM((4, 2 * rows, sub), bf16),
            pltpu.VMEM((4, 2 * rows, sub), bf16),
            pltpu.VMEM((4, 2 * rows, sub), bf16),
            pltpu.VMEM((2, 2 * rows, sub), bf16),
            pltpu.VMEM((2, 2 * rows, sub), bf16),
            pltpu.VMEM((4, 2 * rows, sub), bf16),
            pltpu.VMEM((4, 2 * rows, sub), bf16),
            pltpu.VMEM((2, rows, width), bf16),
            pltpu.VMEM((4, 2, rows, sub), bf16),
            pltpu.VMEM((2, 4, rows, sub), bf16),
            pltpu.SemaphoreType.DMA((7,)),
            pltpu.SemaphoreType.DMA((160,)),
            pltpu.SemaphoreType.DMA((160,)),
        ],
        compiler_params=pltpu.CompilerParams(
            collective_id=0, has_side_effects=True, vmem_limit_bytes=56 * 1024 * 1024
        ),
        name="block",
    )(
        timesteps, table, queue, noise_frame, norm_gains,
        w_qkv.reshape(8, eighth, 3 * hs), w_out.reshape(8, hs // 8, width),
    )


def solution(mesh):
    return jax.shard_map(
        body,
        mesh=mesh,
        in_specs=(
            P("frame", ("head", "tok"), None),
            P("frame"),
            P(),
            P(None, "head", None),
            P(),
            P("head", None, None),
            P(("head", "tok"), None),
        ),
        out_specs=P("frame", ("head", "tok"), None),
        check_vma=False,
    )
```

```python
import functools

import jax
import jax.numpy as jnp
from jax import lax
from jax.experimental import pallas as pl
from jax.experimental.pallas import tpu as pltpu
from jax.sharding import PartitionSpec as P

MESH = pl.DeviceIdType.MESH
NX = 4
NY = 4
NZ = 4
OWN, LEFT, RIGHT, OPP = 0, 1, 2, 3


class Place:
    def __init__(self):
        self.frame = lax.axis_index("frame")
        self.head = lax.axis_index("head")
        self.core = lax.axis_index("tok")
        self.x, self.zh = self.head // NZ, self.head % NZ
        self.y, self.zl = self.frame // 2, self.frame % 2

    def to(self, x=0, z=0, y=0, frame=0, flip=False, core=None):
        head = ((self.x + x) % NX) * NZ + (self.zh + z) % NZ
        own = ((self.y + y) % NY) * 2 + self.zl if frame == 0 else self.frame + frame
        tok = self.core if core is None else core
        tok = 1 - tok if flip else tok
        return (own, head, tok)


class Copies:
    def __init__(self, send, recv):
        self.send, self.recv, self.count, self.all = send, recv, 0, {}

    def make(self, name, src, dst, device):
        k = self.count
        self.count += 1
        copy = pltpu.make_async_remote_copy(
            src_ref=src,
            dst_ref=dst,
            send_sem=self.send.at[k],
            recv_sem=self.recv.at[k],
            device_id=device,
            device_id_type=MESH,
        )
        self.all[name] = copy
        return copy

    def start(self, name, src, dst, device):
        self.make(name, src, dst, device).start()

    def got(self, *names):
        for name in names:
            self.all[name].wait_recv()

    def sent(self, skip=()):
        for name, copy in self.all.items():
            if name not in skip:
                copy.wait_send()


def greet(devices, count):
    barrier = pltpu.get_barrier_semaphore()
    for device in devices:
        pl.semaphore_signal(barrier, inc=1, device_id=device, device_id_type=MESH)
    pl.semaphore_wait(barrier, count)


class Gather:
    def __init__(self, tag, copies, me, ring, source, held, half, whole):
        self.tag, self.copies, self.me, self.ring = tag, copies, me, ring
        self.source, self.held, self.half, self.whole = source, held, half, whole
        self.mine = me.core * NY + me.y
        self.left = me.core * NY + (me.y + NY - 1) % NY
        self.right = me.core * NY + (me.y + 1) % NY
        self.far = me.core * NY + (me.y + 2) % NY

    def part(self, rel, eighth, which):
        return self.half(self.held, rel, eighth, which)

    def go(self, name, src, dst, device):
        self.copies.start(self.tag + name, src, dst, device)

    def got(self, *names):
        self.copies.got(*[self.tag + name for name in names])

    def ring_start(self):
        e = self.mine
        self.go("r", self.source(e), self.whole(self.held, LEFT, e), self.me.to(**{self.ring: 1}))
        self.go("l", self.source(e), self.whole(self.held, RIGHT, e), self.me.to(**{self.ring: -1}))

    def ring_relay(self):
        e = self.mine
        self.got("r")
        self.go("rr", self.part(LEFT, e, 0), self.part(OPP, e, 0), self.me.to(**{self.ring: 1}))
        self.y_start(LEFT)
        self.got("l")
        self.go("ll", self.part(RIGHT, e, 1), self.part(OPP, e, 1), self.me.to(**{self.ring: -1}))
        self.y_start(RIGHT)

    def ring_end(self):
        self.got("rr", "ll")
        self.y_start(OPP)

    def y_start(self, rel):
        n, e = str(rel), self.mine
        self.go("yr" + n, self.whole(self.held, rel, e), self.whole(self.held, rel, e), self.me.to(y=1))
        self.go("yl" + n, self.whole(self.held, rel, e), self.whole(self.held, rel, e), self.me.to(y=-1))
        self.go("s0" + n, self.whole(self.held, rel, e), self.whole(self.held, rel, e), self.me.to(flip=True))

    def y_relay(self, rel):
        n = str(rel)
        self.got("yr" + n)
        e = self.left
        self.go("yrr" + n, self.part(rel, e, 0), self.part(rel, e, 0), self.me.to(y=1))
        self.go("s1" + n, self.whole(self.held, rel, e), self.whole(self.held, rel, e), self.me.to(flip=True))
        self.got("yl" + n)
        e = self.right
        self.go("yll" + n, self.part(rel, e, 1), self.part(rel, e, 1), self.me.to(y=-1))
        self.go("s2" + n, self.whole(self.held, rel, e), self.whole(self.held, rel, e), self.me.to(flip=True))

    def y_end(self, rel):
        n = str(rel)
        self.got("yrr" + n, "yll" + n)
        e = self.far
        self.go("s3" + n, self.whole(self.held, rel, e), self.whole(self.held, rel, e), self.me.to(flip=True))

    def done(self, rel):
        n = str(rel)
        self.got("s0" + n, "s1" + n, "s2" + n, "s3" + n)


class Direct:
    def __init__(self, tag, copies, me, source, held, count, cols):
        self.tag, self.copies, self.me, self.count, self.cols = tag, copies, me, count, cols
        self.source, self.held = source, held
        self.quad = pl.ds(me.core * NY, NY)
        self.low = count // 2

    def rows(self, rel, first, count):
        return self.held.at[rel, self.quad, pl.ds(first, count), self.cols]

    def go(self, name, src, dst, device):
        self.copies.start(self.tag + name, src, dst, device)

    def got(self, *names):
        self.copies.got(*[self.tag + name for name in names])

    def start(self):
        source = self.source.at[self.quad, pl.ds(0, self.count), self.cols]
        self.go("r", source, self.rows(LEFT, 0, self.count), self.me.to(x=1))
        self.go("l", source, self.rows(RIGHT, 0, self.count), self.me.to(x=-1))

    def beside(self, rel):
        part = self.rows(rel, 0, self.count)
        self.go("s" + str(rel), part, part, self.me.to(flip=True))

    def relay(self):
        low, high = self.low, self.count - self.low
        self.got("r")
        self.go("rr", self.rows(LEFT, 0, low), self.rows(OPP, 0, low), self.me.to(x=1))
        self.beside(LEFT)
        self.got("l")
        self.go("ll", self.rows(RIGHT, low, high), self.rows(OPP, low, high), self.me.to(x=-1))
        self.beside(RIGHT)

    def end(self):
        self.got("rr", "ll")
        self.beside(OPP)


def rms_scale(values, gain):
    return values * lax.rsqrt(jnp.mean(values * values, axis=-1, keepdims=True) + 1e-06) * gain


def block_kernel(
    steps_ref, mod_hbm, queue_hbm, noise_hbm, gains_hbm, w_hbm, wo_hbm, out_hbm,
    mod, queue_ref, gains_ref, xg, wg, sbk, rbk, sbq, rbq, kvb, kt, vx, oa, top, attn_s, attn_g, wo, po, pr_s, pl_s, rl, rr, fl, fr,
    qb, ob, ou, local, send, recv,
):
    me = Place()
    core, frame = me.core, me.frame
    frames = lax.axis_size("frame")
    rows, width = queue_ref.shape[1:]
    hs = gains_ref.shape[1]
    bf16, f32 = jnp.bfloat16, jnp.float32
    half = width // 2
    tokens = NZ * rows
    keys = NX * 2 * tokens
    beside = frame + 2 * core - 1
    has_beside = jnp.logical_and(beside >= 0, beside < frames)
    after = (frame + 1) % frames
    before = (frame + frames - 1) % frames
    back = {LEFT: RIGHT, RIGHT: LEFT, OPP: OPP}
    shift = {LEFT: -1, RIGHT: 1, OPP: 2}

    mod_copy = pltpu.make_async_copy(mod_hbm, mod, local.at[6])
    mod_copy.start()
    queue_copy = pltpu.make_async_copy(queue_hbm, queue_ref, local.at[7])
    queue_copy.start()
    gains_copy = pltpu.make_async_copy(gains_hbm, gains_ref, local.at[8])
    gains_copy.start()
    partners = [me.to(flip=True)]
    for step in (1, -1, 2):
        partners += [me.to(x=step), me.to(x=step, flip=True), me.to(z=step)]
    partners += [me.to(y=1), me.to(y=-1)]
    partners += [(before, me.head, 1)]
    barrier = pltpu.get_barrier_semaphore()
    for device in partners:
        pl.semaphore_signal(barrier, inc=1, device_id=device, device_id_type=MESH)

    @pl.when(core == 1)
    def _():
        for tok in range(2):
            pl.semaphore_signal(
                barrier, inc=1, device_id=(after, me.head, tok), device_id_type=MESH
            )

    queue_copy.wait()
    mod_copy.wait()
    for slot in range(2):
        level = pl.ds(steps_ref[slot], 1)
        x = queue_ref[slot].astype(f32)
        centred = x - jnp.mean(x, axis=-1, keepdims=True)
        normed = centred * lax.rsqrt(jnp.mean(centred * centred, axis=-1, keepdims=True) + 1e-06)
        xg[OWN, slot * rows : (slot + 1) * rows, :] = (
            normed * (1.0 + mod[1, level, :]) + mod[0, level, :]
        ).astype(bf16)
    pl.semaphore_wait(barrier, len(partners) + 2 * core)

    copies = Copies(send, recv)
    rows_in = wg.shape[2]
    direct = rows_in // 3 // 32 * 32
    part = (rows_in - direct) // 2

    def gather(tag, cols):
        return Gather(
            tag, copies, me, "x", (lambda e: w_hbm.at[e, pl.ds(direct, 2 * part), cols]), wg,
            lambda ref, rel, e, which: ref.at[rel, e, pl.ds(direct + which * part, part), cols],
            lambda ref, rel, e: ref.at[rel, e, pl.ds(direct, 2 * part), cols],
        )

    q_cols, kv_cols = pl.ds(0, hs), pl.ds(hs, 2 * hs)
    wk, wq = gather("wk", kv_cols), gather("wq", q_cols)
    dk = Direct("dk", copies, me, w_hbm, wg, direct, kv_cols)
    dq = Direct("dq", copies, me, w_hbm, wg, direct, q_cols)
    wk.ring_start()
    own_w = pltpu.make_async_copy(w_hbm, wg.at[OWN], local.at[0])
    own_w.start()
    own_wo = pltpu.make_async_copy(wo_hbm, wo.at[OWN], local.at[1])
    own_wo.start()
    first, second = pl.ds(0, rows), pl.ds(rows, rows)
    copies.start("zr0", xg.at[OWN, first], xg.at[LEFT, first], me.to(z=1))
    copies.start("zl1", xg.at[OWN, second], xg.at[RIGHT, second], me.to(z=-1))
    copies.start("zr1", xg.at[OWN, second], xg.at[LEFT, second], me.to(z=1))
    copies.start("zl0", xg.at[OWN, first], xg.at[RIGHT, first], me.to(z=-1))
    copies.start("qs", queue_hbm.at[1 - core], qb.at[core], me.to(flip=True))

    wk.ring_relay()
    dk.start()
    wq.ring_start()
    copies.got("zr0")
    copies.start("zrr", xg.at[LEFT, first], xg.at[OPP, first], me.to(z=1))
    copies.got("zl1")
    copies.start("zll", xg.at[RIGHT, second], xg.at[OPP, second], me.to(z=-1))
    outs = Gather(
        "o", copies, me, "z", (lambda e: wo_hbm.at[e]), wo,
        lambda ref, rel, e, which: ref.at[rel, e, :, pl.ds(which * half, half)],
        lambda ref, rel, e: ref.at[rel, e],
    )
    outs.ring_start()
    wk.ring_end()
    wk.y_relay(LEFT)
    wk.y_relay(RIGHT)
    dk.relay()
    wq.ring_relay()
    dq.start()
    wk.y_relay(OPP)
    wk.y_end(LEFT)
    wk.y_end(RIGHT)
    dk.end()
    gains_copy.wait()
    q_gain = gains_ref[0:1, :] * f32(1.4426950408889634 / hs**0.5)
    k_gain = gains_ref[1:2, :]
    groups = (pl.ds(0, NZ - 1), pl.ds(NZ - 1, 1))
    sizes = (NZ - 1, 1)

    def send_rows(tag, sent, home, rel, which):
        if rel == OWN:
            copies.start(
                "a" + tag, sent.at[OWN, 1 - core, which], home.at[core, which], me.to(flip=True)
            )
            home[core, which] = sent[OWN, core, which]
            return
        spot = home.at[back[rel] * 2 + core, which]
        copies.start("a" + tag, sent.at[rel, core, which], spot, me.to(x=shift[rel]))
        copies.start(
            "b" + tag, sent.at[rel, 1 - core, which], spot, me.to(x=shift[rel], flip=True)
        )

    def project_kv(rel, group):
        which, count = groups[group], sizes[group]
        xs = xg[which].reshape(count * 2 * rows, width)
        w = wg[rel, :, :, hs:].reshape(width, 2 * hs)
        kv = jnp.dot(xs, w, preferred_element_type=f32)
        k = rms_scale(kv[:, :hs], k_gain)
        out = jnp.concatenate([k, kv[:, hs:]], axis=-1).astype(bf16)
        out = out.reshape(count, 2, rows, 2 * hs)
        for slot in range(2):
            sbk[rel, slot, which] = out[:, slot]
        send_rows(f"k{rel}{group}", sbk, rbk, rel, which)

    def project_q(rel):
        xs = xg[...].reshape(NZ * 2 * rows, width)
        w = wg[rel, :, :, :hs].reshape(width, hs)
        q = rms_scale(jnp.dot(xs, w, preferred_element_type=f32), q_gain)
        out = q.astype(bf16).reshape(NZ, 2, rows, hs)
        for slot in range(2):
            sbq[rel, slot] = out[:, slot]
        send_rows(f"q{rel}", sbq, rbq, rel, pl.ds(0, NZ))

    def share(rel, group):
        n = f"{rel}{group}"
        copies.got("ak" + n)
        if rel != OWN:
            copies.got("bk" + n)
        spot = OWN if rel == OWN else back[rel]
        pair = pl.ds(spot * 2, 2)
        src = rbk.at[pair, groups[group]]
        side = copies.make("kv" + n, src, kvb.at[1, pair, groups[group]], (beside, me.head, 1 - core))

        @pl.when(has_beside)
        def _():
            side.start()

        copies.start("ks" + n, src, kvb.at[0, pair, groups[group]], me.to(flip=True))

    own_w.wait()
    copies.got("zr1", "zl0")
    project_kv(OWN, 0)
    wq.ring_end()
    wk.done(LEFT)
    dk.got("s1")
    project_kv(LEFT, 0)
    wk.done(RIGHT)
    dk.got("s2")
    project_kv(RIGHT, 0)
    share(OWN, 0)
    wk.y_end(OPP)
    wq.y_relay(LEFT)
    dq.relay()
    wk.done(OPP)
    dk.got("s3")
    project_kv(OPP, 0)
    wq.y_relay(RIGHT)
    share(LEFT, 0)
    share(RIGHT, 0)
    wq.y_relay(OPP)
    wq.y_end(LEFT)
    copies.got("zrr", "zll")
    for rel in range(4):
        project_kv(rel, 1)
    outs.ring_relay()
    share(OPP, 0)
    dq.end()
    wq.y_end(RIGHT)
    wq.y_end(OPP)
    project_q(OWN)
    share(OWN, 1)
    wq.done(LEFT)
    dq.got("s1")
    project_q(LEFT)
    share(LEFT, 1)
    wq.done(RIGHT)
    dq.got("s2")
    project_q(RIGHT)
    share(RIGHT, 1)
    wq.done(OPP)
    dq.got("s3")
    project_q(OPP)
    share(OPP, 1)
    names = [f"{rel}{group}" for rel in range(4) for group in range(2)]

    ones = jnp.ones((keys, hs), bf16)

    def take(which, kv):
        kt[which] = kv[:, :hs].T
        vx[which, :, :hs] = kv[:, hs:]
        vx[which, :, hs:] = ones

    take(0, rbk[...].reshape(keys, 2 * hs))
    outs.ring_end()
    copies.got(*["ks" + n for n in names])
    take(1, kvb[0].reshape(keys, 2 * hs))

    block = 2 * tokens

    def queries(i):
        return rbq[pl.ds(2 * i, 2)].reshape(block, hs)

    def first_part(rx):
        q = queries(rx)
        scores = [jnp.dot(q, kt[j], preferred_element_type=f32) for j in range(2)]
        peak = jnp.maximum(
            jnp.max(scores[0], axis=-1, keepdims=True), jnp.max(scores[1], axis=-1, keepdims=True)
        )
        total = jnp.zeros((block, 2 * hs), f32)
        for j in range(2):
            p = jnp.exp2(scores[j] - peak).astype(bf16)
            total += jnp.dot(p, vx[j], preferred_element_type=f32)
        oa[rx] = total
        top[rx] = jnp.broadcast_to(peak, (block, hs))

    def attend(rx):
        @pl.when(has_beside)
        def _():
            s = jnp.dot(queries(rx), kt[2], preferred_element_type=f32)
            old = top[rx][:, :1]
            peak = jnp.maximum(old, jnp.max(s, axis=-1, keepdims=True))
            p = jnp.exp2(s - peak).astype(bf16)
            oa[rx] = oa[rx] * jnp.exp2(old - peak) + jnp.dot(
                p, vx[2], preferred_element_type=f32
            )

        o = oa[rx]
        attn = (o[:, :hs] / o[:, hs:]).astype(bf16).reshape(2, NZ, rows, hs)
        attn_g[rx, OWN] = attn[:, OWN].reshape(2 * rows, hs)
        for rz in (LEFT, RIGHT, OPP):
            attn_s[rx, rz] = attn[:, rz].reshape(2 * rows, hs)
            copies.start(
                f"t{rx}{rz}", attn_s.at[rx, rz], attn_g.at[rx, back[rz]], me.to(z=shift[rz])
            )

    def contribution(rx):
        copies.got(*[f"t{rx}{rz}" for rz in (LEFT, RIGHT, OPP)])
        a = jnp.concatenate([attn_g[rx, rz] for rz in range(NZ)], axis=-1)
        return jnp.dot(a, wo[...].reshape(NZ * hs, width), preferred_element_type=f32)

    copies.got("aq0")
    for rel in (LEFT, RIGHT, OPP):
        copies.got(f"aq{rel}", f"bq{rel}")
    first_part(OPP)
    first_part(RIGHT)
    first_part(LEFT)
    first_part(OWN)
    for rel in (LEFT, RIGHT, OPP):
        outs.y_relay(rel)

    @pl.when(has_beside)
    def _():
        for n in names:
            copies.got("kv" + n)
        take(2, kvb[1].reshape(keys, 2 * hs))

    attend(OPP)
    attend(RIGHT)
    attend(LEFT)
    for rel in (LEFT, RIGHT, OPP):
        outs.y_end(rel)
    own_wo.wait()
    for rel in (LEFT, RIGHT, OPP):
        outs.done(rel)

    sub = half // 2
    p = contribution(OPP).astype(bf16)
    for j in range(2):
        po[j] = p[:, j * sub : (j + 1) * sub]
        po[2 + j] = p[:, half + j * sub : half + (j + 1) * sub]
        copies.start(f"rl{j}", po.at[j], rl.at[j], me.to(x=1))
        copies.start(f"rr{j}", po.at[2 + j], rr.at[j], me.to(x=-1))
    attend(OWN)

    right = contribution(RIGHT)
    for j in range(2):
        pr_s[2 + j] = right[:, half + j * sub : half + (j + 1) * sub].astype(bf16)
        copies.start(f"fl{2 + j}", pr_s.at[2 + j], fl.at[2 + j], me.to(x=1))
    left = contribution(LEFT)
    for j in range(2):
        pl_s[j] = left[:, j * sub : (j + 1) * sub].astype(bf16)
        copies.start(f"fr{j}", pl_s.at[j], fr.at[j], me.to(x=-1))
    for j in range(2):
        copies.got(f"rl{j}")
        pr_s[j] = (right[:, j * sub : (j + 1) * sub] + rl[j].astype(f32)).astype(bf16)
        copies.start(f"fl{j}", pr_s.at[j], fl.at[j], me.to(x=1))
        copies.got(f"rr{j}")
        pl_s[2 + j] = (
            left[:, half + j * sub : half + (j + 1) * sub] + rr[j].astype(f32)
        ).astype(bf16)
        copies.start(f"fr{2 + j}", pl_s.at[2 + j], fr.at[2 + j], me.to(x=-1))

    p = contribution(OWN)
    copies.got("qs")
    qb[core] = queue_ref[core]
    gate = mod[2, pl.ds(steps_ref[core], 1), :]
    sends_on = jnp.logical_and(core == 1, frame < frames - 1)
    near, next0, next1, kept = {}, {}, {}, {}
    noise_copy = pltpu.make_async_copy(noise_hbm, out_hbm.at[0], local.at[9])

    @pl.when(frame == 0)
    def _():
        noise_copy.start()

    for j in range(2):
        copies.got(f"fl{j}", f"fr{j}", f"fl{2 + j}", f"fr{2 + j}")
        for h in (j, 2 + j):
            cols = slice(h * sub, (h + 1) * sub)
            proj = p[:, cols] + fl[h].astype(f32) + fr[h].astype(f32)
            for tok in range(2):
                ob[h, tok] = (
                    qb[tok, :, cols].astype(f32)
                    + gate[:, cols] * proj[tok * rows : (tok + 1) * rows]
                ).astype(bf16)
        for h in (j, 2 + j):
            cols = pl.ds(h * sub, sub)
            kept[h] = pltpu.make_async_copy(ob.at[h, 0], out_hbm.at[1, :, cols], local.at[10 + h])
            near[h] = copies.make(f"o{h}", ob.at[h, 1], ou.at[1, h], me.to(flip=True))
            next0[h] = copies.make(f"n{h}", ob.at[h, 0], ou.at[0, h], (after, me.head, 0))
            next1[h] = pltpu.make_async_remote_copy(
                src_ref=ob.at[h, 1], dst_ref=ou.at[0, h],
                send_sem=local.at[2 + h], recv_sem=recv.at[copies.count - 1],
                device_id=(after, me.head, 1), device_id_type=MESH,
            )

        @pl.when(core == 0)
        def _():
            for h in (j, 2 + j):
                near[h].start()
                kept[h].start()

        @pl.when(sends_on)
        def _():
            for h in (j, 2 + j):
                next0[h].start()
                next1[h].start()

    def keep(slot, h):
        cols = pl.ds(h * sub, sub)
        return pltpu.make_async_copy(
            ou.at[slot, h], out_hbm.at[slot, :, cols], local.at[14 + 4 * slot + h]
        )

    @pl.when(core == 1)
    def _():
        for h in range(4):
            near[h].wait_recv()
            keep(1, h).start()

    @pl.when(frame > 0)
    def _():
        for h in range(4):
            next0[h].wait_recv()
            keep(0, h).start()

    @pl.when(core == 0)
    def _():
        for h in range(4):
            near[h].wait_send()
            kept[h].wait()

    @pl.when(core == 1)
    def _():
        for h in range(4):
            keep(1, h).wait()

    @pl.when(frame > 0)
    def _():
        for h in range(4):
            keep(0, h).wait()

    @pl.when(frame == 0)
    def _():
        noise_copy.wait()

    @pl.when(sends_on)
    def _():
        for h in range(4):
            next0[h].wait_send()
            next1[h].wait_send()

    @pl.when(has_beside)
    def _():
        for n in names:
            copies.all["kv" + n].wait_send()

    copies.sent(skip=[f"{t}{h}" for t in "on" for h in range(4)] + ["kv" + n for n in names])


def body(queue, timesteps, mod_table, w_qkv, norm_gains, w_out, noise_frame):
    slots, rows, width = queue.shape
    hs = w_out.shape[1]
    bf16, f32 = jnp.bfloat16, jnp.float32
    hbm = pl.BlockSpec(memory_space=pl.ANY)
    smem = pl.BlockSpec(memory_space=pltpu.SMEM)
    tokens = NZ * rows
    keys = NX * 2 * tokens
    eighth = width // 8
    half = width // 2
    sub = half // 2
    table = jnp.transpose(mod_table, (1, 0, 2))
    return pl.pallas_call(
        block_kernel,
        out_shape=jax.ShapeDtypeStruct(queue.shape, bf16),
        in_specs=[smem] + [hbm] * 6,
        out_specs=hbm,
        scratch_shapes=[
            pltpu.VMEM(table.shape, f32),
            pltpu.VMEM(queue.shape, bf16),
            pltpu.VMEM(norm_gains.shape, f32),
            pltpu.VMEM((NZ, 2 * rows, width), bf16),
            pltpu.VMEM((NX, 8, eighth, 3 * hs), bf16),
            pltpu.VMEM((NX, 2, NZ, rows, 2 * hs), bf16),
            pltpu.VMEM((NX * 2, NZ, rows, 2 * hs), bf16),
            pltpu.VMEM((NX, 2, NZ, rows, hs), bf16),
            pltpu.VMEM((NX * 2, NZ, rows, hs), bf16),
            pltpu.VMEM((2, NX * 2, NZ, rows, 2 * hs), bf16),
            pltpu.VMEM((3, hs, keys), bf16),
            pltpu.VMEM((3, keys, 2 * hs), bf16),
            pltpu.VMEM((NX, 2 * tokens, 2 * hs), f32),
            pltpu.VMEM((NX, 2 * tokens, hs), f32),
            pltpu.VMEM((NX, NZ, 2 * rows, hs), bf16),
            pltpu.VMEM((NX, NZ, 2 * rows, hs), bf16),
            pltpu.VMEM((NZ, 8, hs // 8, width), bf16),
            pltpu.VMEM((4, 2 * rows, sub), bf16),
            pltpu.VMEM((4, 2 * rows, sub), bf16),
            pltpu.VMEM((4, 2 * rows, sub), bf16),
            pltpu.VMEM((2, 2 * rows, sub), bf16),
            pltpu.VMEM((2, 2 * rows, sub), bf16),
            pltpu.VMEM((4, 2 * rows, sub), bf16),
            pltpu.VMEM((4, 2 * rows, sub), bf16),
            pltpu.VMEM((2, rows, width), bf16),
            pltpu.VMEM((4, 2, rows, sub), bf16),
            pltpu.VMEM((2, 4, rows, sub), bf16),
            pltpu.SemaphoreType.DMA((22,)),
            pltpu.SemaphoreType.DMA((200,)),
            pltpu.SemaphoreType.DMA((200,)),
        ],
        compiler_params=pltpu.CompilerParams(
            collective_id=0, has_side_effects=True, vmem_limit_bytes=56 * 1024 * 1024
        ),
        name="block",
    )(
        timesteps, table, queue, noise_frame, norm_gains,
        w_qkv.reshape(8, eighth, 3 * hs), w_out.reshape(8, hs // 8, width),
    )


def solution(mesh):
    return jax.shard_map(
        body,
        mesh=mesh,
        in_specs=(
            P("frame", ("head", "tok"), None),
            P("frame"),
            P(),
            P(None, "head", None),
            P(),
            P("head", None, None),
            P(("head", "tok"), None),
        ),
        out_specs=P("frame", ("head", "tok"), None),
        check_vma=False,
    )
```

```python
import functools

import jax
import jax.numpy as jnp
from jax import lax
from jax.experimental import pallas as pl
from jax.experimental.pallas import tpu as pltpu
from jax.sharding import PartitionSpec as P

MESH = pl.DeviceIdType.MESH
NX = 4
NY = 4
NZ = 4
OWN, LEFT, RIGHT, OPP = 0, 1, 2, 3


class Place:
    def __init__(self):
        self.frame = lax.axis_index("frame")
        self.head = lax.axis_index("head")
        self.core = lax.axis_index("tok")
        self.x, self.zh = self.head // NZ, self.head % NZ
        self.y, self.zl = self.frame // 2, self.frame % 2

    def to(self, x=0, z=0, y=0, frame=0, flip=False, core=None):
        head = ((self.x + x) % NX) * NZ + (self.zh + z) % NZ
        own = ((self.y + y) % NY) * 2 + self.zl if frame == 0 else self.frame + frame
        tok = self.core if core is None else core
        tok = 1 - tok if flip else tok
        return (own, head, tok)


class Copies:
    def __init__(self, send, recv):
        self.send, self.recv, self.count, self.all = send, recv, 0, {}

    def make(self, name, src, dst, device):
        k = self.count
        self.count += 1
        copy = pltpu.make_async_remote_copy(
            src_ref=src,
            dst_ref=dst,
            send_sem=self.send.at[k],
            recv_sem=self.recv.at[k],
            device_id=device,
            device_id_type=MESH,
        )
        self.all[name] = copy
        return copy

    def start(self, name, src, dst, device):
        self.make(name, src, dst, device).start()

    def got(self, *names):
        for name in names:
            self.all[name].wait_recv()

    def sent(self, skip=()):
        for name, copy in self.all.items():
            if name not in skip:
                copy.wait_send()


def greet(devices, count):
    barrier = pltpu.get_barrier_semaphore()
    for device in devices:
        pl.semaphore_signal(barrier, inc=1, device_id=device, device_id_type=MESH)
    pl.semaphore_wait(barrier, count)


class Gather:
    def __init__(self, tag, copies, me, ring, source, held, half, whole):
        self.tag, self.copies, self.me, self.ring = tag, copies, me, ring
        self.source, self.held, self.half, self.whole = source, held, half, whole
        self.mine = me.core * NY + me.y
        self.left = me.core * NY + (me.y + NY - 1) % NY
        self.right = me.core * NY + (me.y + 1) % NY
        self.far = me.core * NY + (me.y + 2) % NY

    def part(self, rel, eighth, which):
        return self.half(self.held, rel, eighth, which)

    def go(self, name, src, dst, device):
        self.copies.start(self.tag + name, src, dst, device)

    def got(self, *names):
        self.copies.got(*[self.tag + name for name in names])

    def ring_start(self):
        e = self.mine
        self.go("r", self.source(e), self.whole(self.held, LEFT, e), self.me.to(**{self.ring: 1}))
        self.go("l", self.source(e), self.whole(self.held, RIGHT, e), self.me.to(**{self.ring: -1}))

    def ring_relay(self):
        e = self.mine
        self.got("r")
        self.go("rr", self.part(LEFT, e, 0), self.part(OPP, e, 0), self.me.to(**{self.ring: 1}))
        self.y_start(LEFT)
        self.got("l")
        self.go("ll", self.part(RIGHT, e, 1), self.part(OPP, e, 1), self.me.to(**{self.ring: -1}))
        self.y_start(RIGHT)

    def ring_end(self):
        self.got("rr", "ll")
        self.y_start(OPP)

    def y_start(self, rel):
        n, e = str(rel), self.mine
        self.go("yr" + n, self.whole(self.held, rel, e), self.whole(self.held, rel, e), self.me.to(y=1))
        self.go("yl" + n, self.whole(self.held, rel, e), self.whole(self.held, rel, e), self.me.to(y=-1))
        self.go("s0" + n, self.whole(self.held, rel, e), self.whole(self.held, rel, e), self.me.to(flip=True))

    def y_relay(self, rel):
        n = str(rel)
        self.got("yr" + n)
        e = self.left
        self.go("yrr" + n, self.part(rel, e, 0), self.part(rel, e, 0), self.me.to(y=1))
        self.go("s1" + n, self.whole(self.held, rel, e), self.whole(self.held, rel, e), self.me.to(flip=True))
        self.got("yl" + n)
        e = self.right
        self.go("yll" + n, self.part(rel, e, 1), self.part(rel, e, 1), self.me.to(y=-1))
        self.go("s2" + n, self.whole(self.held, rel, e), self.whole(self.held, rel, e), self.me.to(flip=True))

    def y_end(self, rel):
        n = str(rel)
        self.got("yrr" + n, "yll" + n)
        e = self.far
        self.go("s3" + n, self.whole(self.held, rel, e), self.whole(self.held, rel, e), self.me.to(flip=True))

    def done(self, rel):
        n = str(rel)
        self.got("s0" + n, "s1" + n, "s2" + n, "s3" + n)


class PairGather(Gather):
    def __init__(self, *args):
        super().__init__(*args)
        me = self.me
        twin = me.y * 2 + 1 - me.zl
        step = 2 * me.zl - 1
        self.twin = (twin, me.head, me.core)
        self.hop = (twin, me.x * NZ + (me.zh + step + NZ) % NZ, me.core)
        self.got_first, self.got_second = 1 + me.zl, 2 - me.zl

    def ring_start(self):
        e = self.mine
        self.go("r", self.source(e), self.whole(self.held, self.got_second, e), self.hop)

    def ring_relay(self):
        self.got("r")
        part = self.whole(self.held, self.got_first, self.mine)
        self.go("x", part, part, self.twin)

    def ring_last(self):
        e = self.mine
        self.got("x")
        self.go("rr", self.whole(self.held, self.got_second, e), self.whole(self.held, OPP, e), self.hop)
        self.y_start(LEFT)
        self.y_start(RIGHT)

    def ring_end(self):
        self.got("rr")
        self.y_start(OPP)


class Direct:
    def __init__(self, tag, copies, me, source, held, count, cols):
        self.tag, self.copies, self.me, self.count, self.cols = tag, copies, me, count, cols
        self.source, self.held = source, held
        self.quad = pl.ds(me.core * NY, NY)
        self.low = count // 2

    def rows(self, rel, first, count):
        return self.held.at[rel, self.quad, pl.ds(first, count), self.cols]

    def go(self, name, src, dst, device):
        self.copies.start(self.tag + name, src, dst, device)

    def got(self, *names):
        self.copies.got(*[self.tag + name for name in names])

    def start(self):
        source = self.source.at[self.quad, pl.ds(0, self.count), self.cols]
        self.go("r", source, self.rows(LEFT, 0, self.count), self.me.to(x=1))
        self.go("l", source, self.rows(RIGHT, 0, self.count), self.me.to(x=-1))

    def beside(self, rel):
        part = self.rows(rel, 0, self.count)
        self.go("s" + str(rel), part, part, self.me.to(flip=True))

    def relay(self):
        low, high = self.low, self.count - self.low
        self.got("r")
        self.go("rr", self.rows(LEFT, 0, low), self.rows(OPP, 0, low), self.me.to(x=1))
        self.beside(LEFT)
        self.got("l")
        self.go("ll", self.rows(RIGHT, low, high), self.rows(OPP, low, high), self.me.to(x=-1))
        self.beside(RIGHT)

    def end(self):
        self.got("rr", "ll")
        self.beside(OPP)


def rms_scale(values, gain):
    return values * lax.rsqrt(jnp.mean(values * values, axis=-1, keepdims=True) + 1e-06) * gain


def block_kernel(
    steps_ref, mod_hbm, queue_hbm, noise_hbm, gains_hbm, w_hbm, wo_hbm, out_hbm,
    mod, queue_ref, gains_ref, xg, wg, sbk, rbk, sbq, rbq, kvb, kt, vx, oa, top, attn_s, attn_g, wo, po, pr_s, pl_s, rl, rr, fl, fr,
    qb, ob, ou, local, send, recv,
):
    me = Place()
    core, frame = me.core, me.frame
    frames = lax.axis_size("frame")
    rows, width = queue_ref.shape[1:]
    hs = gains_ref.shape[1]
    bf16, f32 = jnp.bfloat16, jnp.float32
    half = width // 2
    tokens = NZ * rows
    keys = NX * 2 * tokens
    beside = frame + 2 * core - 1
    has_beside = jnp.logical_and(beside >= 0, beside < frames)
    after = (frame + 1) % frames
    before = (frame + frames - 1) % frames
    back = {LEFT: RIGHT, RIGHT: LEFT, OPP: OPP}
    shift = {LEFT: -1, RIGHT: 1, OPP: 2}

    mod_copy = pltpu.make_async_copy(mod_hbm, mod, local.at[6])
    mod_copy.start()
    queue_copy = pltpu.make_async_copy(queue_hbm, queue_ref, local.at[7])
    queue_copy.start()
    gains_copy = pltpu.make_async_copy(gains_hbm, gains_ref, local.at[8])
    gains_copy.start()
    copies = Copies(send, recv)
    outs = PairGather(
        "o", copies, me, "z", (lambda e: wo_hbm.at[e]), wo,
        lambda ref, rel, e, which: ref.at[rel, e, :, pl.ds(which * half, half)],
        lambda ref, rel, e: ref.at[rel, e],
    )
    partners = [me.to(flip=True)]
    for step in (1, -1, 2):
        partners += [me.to(x=step), me.to(x=step, flip=True), me.to(z=step)]
    partners += [me.to(y=1), me.to(y=-1)]
    partners += [(before, me.head, 1), outs.twin, outs.hop]
    barrier = pltpu.get_barrier_semaphore()
    for device in partners:
        pl.semaphore_signal(barrier, inc=1, device_id=device, device_id_type=MESH)

    @pl.when(core == 1)
    def _():
        for tok in range(2):
            pl.semaphore_signal(
                barrier, inc=1, device_id=(after, me.head, tok), device_id_type=MESH
            )

    queue_copy.wait()
    mod_copy.wait()
    for slot in range(2):
        level = pl.ds(steps_ref[slot], 1)
        x = queue_ref[slot].astype(f32)
        centred = x - jnp.mean(x, axis=-1, keepdims=True)
        normed = centred * lax.rsqrt(jnp.mean(centred * centred, axis=-1, keepdims=True) + 1e-06)
        xg[OWN, slot * rows : (slot + 1) * rows, :] = (
            normed * (1.0 + mod[1, level, :]) + mod[0, level, :]
        ).astype(bf16)
    pl.semaphore_wait(barrier, len(partners) + 2 * core)

    rows_in = wg.shape[2]

    q_cols, kv_cols = pl.ds(0, hs), pl.ds(hs, 2 * hs)

    def gather(tag, cols, direct):
        part = (rows_in - direct) // 2
        ringed = Gather(
            "w" + tag, copies, me, "x",
            (lambda e: w_hbm.at[e, pl.ds(direct, 2 * part), cols]), wg,
            lambda ref, rel, e, which: ref.at[rel, e, pl.ds(direct + which * part, part), cols],
            lambda ref, rel, e: ref.at[rel, e, pl.ds(direct, 2 * part), cols],
        )
        return ringed, Direct("d" + tag, copies, me, w_hbm, wg, direct, cols)

    wk, dk = gather("k", kv_cols, rows_in * 5 // 12)
    wq, dq = gather("q", q_cols, rows_in // 2)
    wk.ring_start()
    own_w = pltpu.make_async_copy(w_hbm, wg.at[OWN], local.at[0])
    own_w.start()
    own_wo = pltpu.make_async_copy(wo_hbm, wo.at[OWN], local.at[1])
    own_wo.start()
    first, second = pl.ds(0, rows), pl.ds(rows, rows)
    copies.start("zr0", xg.at[OWN, first], xg.at[LEFT, first], me.to(z=1))
    copies.start("zl1", xg.at[OWN, second], xg.at[RIGHT, second], me.to(z=-1))
    copies.start("zr1", xg.at[OWN, second], xg.at[LEFT, second], me.to(z=1))
    copies.start("zl0", xg.at[OWN, first], xg.at[RIGHT, first], me.to(z=-1))
    copies.start("qs", queue_hbm.at[1 - core], qb.at[core], me.to(flip=True))

    wk.ring_relay()
    dk.start()
    wq.ring_start()
    copies.got("zr0")
    copies.start("zrr", xg.at[LEFT, first], xg.at[OPP, first], me.to(z=1))
    copies.got("zl1")
    copies.start("zll", xg.at[RIGHT, second], xg.at[OPP, second], me.to(z=-1))
    outs.ring_start()
    wk.ring_end()
    wk.y_relay(LEFT)
    wk.y_relay(RIGHT)
    dk.relay()
    wq.ring_relay()
    dq.start()
    wk.y_relay(OPP)
    wk.y_end(LEFT)
    wk.y_end(RIGHT)
    dk.end()
    gains_copy.wait()
    q_gain = gains_ref[0:1, :] * f32(1.4426950408889634 / hs**0.5)
    k_gain = gains_ref[1:2, :]
    groups = (pl.ds(0, NZ - 1), pl.ds(NZ - 1, 1))
    sizes = (NZ - 1, 1)

    def send_rows(tag, sent, home, rel, which):
        if rel == OWN:
            copies.start(
                "a" + tag, sent.at[OWN, 1 - core, which], home.at[core, which], me.to(flip=True)
            )
            home[core, which] = sent[OWN, core, which]
            return
        spot = home.at[back[rel] * 2 + core, which]
        copies.start("a" + tag, sent.at[rel, core, which], spot, me.to(x=shift[rel]))
        copies.start(
            "b" + tag, sent.at[rel, 1 - core, which], spot, me.to(x=shift[rel], flip=True)
        )

    def project_kv(rel, group):
        which, count = groups[group], sizes[group]
        xs = xg[which].reshape(count * 2 * rows, width)
        w = wg[rel, :, :, hs:].reshape(width, 2 * hs)
        kv = jnp.dot(xs, w, preferred_element_type=f32)
        k = rms_scale(kv[:, :hs], k_gain)
        out = jnp.concatenate([k, kv[:, hs:]], axis=-1).astype(bf16)
        out = out.reshape(count, 2, rows, 2 * hs)
        for slot in range(2):
            sbk[rel, slot, which] = out[:, slot]
        send_rows(f"k{rel}{group}", sbk, rbk, rel, which)

    def project_q(rel):
        xs = xg[...].reshape(NZ * 2 * rows, width)
        w = wg[rel, :, :, :hs].reshape(width, hs)
        q = rms_scale(jnp.dot(xs, w, preferred_element_type=f32), q_gain)
        out = q.astype(bf16).reshape(NZ, 2, rows, hs)
        for slot in range(2):
            sbq[rel, slot] = out[:, slot]
        send_rows(f"q{rel}", sbq, rbq, rel, pl.ds(0, NZ))

    def share(rel, group):
        n = f"{rel}{group}"
        copies.got("ak" + n)
        if rel != OWN:
            copies.got("bk" + n)
        spot = OWN if rel == OWN else back[rel]
        pair = pl.ds(spot * 2, 2)
        src = rbk.at[pair, groups[group]]
        side = copies.make("kv" + n, src, kvb.at[1, pair, groups[group]], (beside, me.head, 1 - core))

        @pl.when(has_beside)
        def _():
            side.start()

        copies.start("ks" + n, src, kvb.at[0, pair, groups[group]], me.to(flip=True))

    own_w.wait()
    copies.got("zr1", "zl0")
    project_kv(OWN, 0)
    wq.ring_end()
    wk.done(LEFT)
    dk.got("s1")
    project_kv(LEFT, 0)
    wk.done(RIGHT)
    dk.got("s2")
    project_kv(RIGHT, 0)
    outs.ring_relay()
    share(OWN, 0)
    wk.y_end(OPP)
    wq.y_relay(LEFT)
    dq.relay()
    wk.done(OPP)
    dk.got("s3")
    project_kv(OPP, 0)
    wq.y_relay(RIGHT)
    share(LEFT, 0)
    share(RIGHT, 0)
    wq.y_relay(OPP)
    wq.y_end(LEFT)
    copies.got("zrr", "zll")
    for rel in range(4):
        project_kv(rel, 1)
    share(OPP, 0)
    outs.ring_last()
    dq.end()
    wq.y_end(RIGHT)
    wq.y_end(OPP)
    project_q(OWN)
    share(OWN, 1)
    wq.done(LEFT)
    dq.got("s1")
    project_q(LEFT)
    share(LEFT, 1)
    wq.done(RIGHT)
    dq.got("s2")
    project_q(RIGHT)
    share(RIGHT, 1)
    wq.done(OPP)
    dq.got("s3")
    project_q(OPP)
    share(OPP, 1)
    outs.ring_end()
    names = [f"{rel}{group}" for rel in range(4) for group in range(2)]

    ones = jnp.ones((keys, hs), bf16)

    def take(which, kv):
        kt[which] = kv[:, :hs].T
        vx[which, :, :hs] = kv[:, hs:]
        vx[which, :, hs:] = ones

    block = 2 * tokens

    def queries(i):
        return rbq[pl.ds(2 * i, 2)].reshape(block, hs)

    def first_part(rx):
        q = queries(rx)
        scores = [jnp.dot(q, kt[j], preferred_element_type=f32) for j in range(2)]
        peak = jnp.maximum(
            jnp.max(scores[0], axis=-1, keepdims=True), jnp.max(scores[1], axis=-1, keepdims=True)
        )
        total = jnp.zeros((block, 2 * hs), f32)
        for j in range(2):
            p = jnp.exp2(scores[j] - peak).astype(bf16)
            total += jnp.dot(p, vx[j], preferred_element_type=f32)
        oa[rx] = total
        top[rx] = jnp.broadcast_to(peak, (block, hs))

    def attend(rx):
        @pl.when(has_beside)
        def _():
            s = jnp.dot(queries(rx), kt[2], preferred_element_type=f32)
            old = top[rx][:, :1]
            peak = jnp.maximum(old, jnp.max(s, axis=-1, keepdims=True))
            p = jnp.exp2(s - peak).astype(bf16)
            oa[rx] = oa[rx] * jnp.exp2(old - peak) + jnp.dot(
                p, vx[2], preferred_element_type=f32
            )

        o = oa[rx]
        attn = (o[:, :hs] / o[:, hs:]).astype(bf16).reshape(2, NZ, rows, hs)
        attn_g[rx, OWN] = attn[:, OWN].reshape(2 * rows, hs)
        for rz in (LEFT, RIGHT, OPP):
            attn_s[rx, rz] = attn[:, rz].reshape(2 * rows, hs)
            copies.start(
                f"t{rx}{rz}", attn_s.at[rx, rz], attn_g.at[rx, back[rz]], me.to(z=shift[rz])
            )

    def contribution(rx):
        copies.got(*[f"t{rx}{rz}" for rz in (LEFT, RIGHT, OPP)])
        a = jnp.concatenate([attn_g[rx, rz] for rz in range(NZ)], axis=-1)
        return jnp.dot(a, wo[...].reshape(NZ * hs, width), preferred_element_type=f32)

    take(0, rbk[...].reshape(keys, 2 * hs))
    copies.got(*["ks" + n for n in names])
    take(1, kvb[0].reshape(keys, 2 * hs))
    copies.got("aq0")
    for rel in (LEFT, RIGHT, OPP):
        copies.got(f"aq{rel}", f"bq{rel}")
    first_part(OPP)
    first_part(RIGHT)
    outs.y_relay(LEFT)
    outs.y_relay(RIGHT)
    first_part(LEFT)
    first_part(OWN)
    outs.y_relay(OPP)

    @pl.when(has_beside)
    def _():
        for n in names:
            copies.got("kv" + n)
        take(2, kvb[1].reshape(keys, 2 * hs))

    attend(OPP)
    attend(RIGHT)
    for rel in (LEFT, RIGHT, OPP):
        outs.y_end(rel)
    attend(LEFT)
    own_wo.wait()
    for rel in (LEFT, RIGHT, OPP):
        outs.done(rel)

    sub = half // 2
    p = contribution(OPP).astype(bf16)
    for j in range(2):
        po[j] = p[:, j * sub : (j + 1) * sub]
        po[2 + j] = p[:, half + j * sub : half + (j + 1) * sub]
        copies.start(f"rl{j}", po.at[j], rl.at[j], me.to(x=1))
        copies.start(f"rr{j}", po.at[2 + j], rr.at[j], me.to(x=-1))
    attend(OWN)

    right = contribution(RIGHT)
    for j in range(2):
        pr_s[2 + j] = right[:, half + j * sub : half + (j + 1) * sub].astype(bf16)
        copies.start(f"fl{2 + j}", pr_s.at[2 + j], fl.at[2 + j], me.to(x=1))
    left = contribution(LEFT)
    for j in range(2):
        pl_s[j] = left[:, j * sub : (j + 1) * sub].astype(bf16)
        copies.start(f"fr{j}", pl_s.at[j], fr.at[j], me.to(x=-1))
    for j in range(2):
        copies.got(f"rl{j}")
        pr_s[j] = (right[:, j * sub : (j + 1) * sub] + rl[j].astype(f32)).astype(bf16)
        copies.start(f"fl{j}", pr_s.at[j], fl.at[j], me.to(x=1))
        copies.got(f"rr{j}")
        pl_s[2 + j] = (
            left[:, half + j * sub : half + (j + 1) * sub] + rr[j].astype(f32)
        ).astype(bf16)
        copies.start(f"fr{2 + j}", pl_s.at[2 + j], fr.at[2 + j], me.to(x=-1))

    p = contribution(OWN)
    copies.got("qs")
    qb[core] = queue_ref[core]
    gate = mod[2, pl.ds(steps_ref[core], 1), :]
    sends_on = jnp.logical_and(core == 1, frame < frames - 1)
    near, next0, next1, kept = {}, {}, {}, {}
    noise_copy = pltpu.make_async_copy(noise_hbm, out_hbm.at[0], local.at[9])

    @pl.when(frame == 0)
    def _():
        noise_copy.start()

    for j in range(2):
        copies.got(f"fl{j}", f"fr{j}", f"fl{2 + j}", f"fr{2 + j}")
        for h in (j, 2 + j):
            cols = slice(h * sub, (h + 1) * sub)
            proj = p[:, cols] + fl[h].astype(f32) + fr[h].astype(f32)
            for tok in range(2):
                ob[h, tok] = (
                    qb[tok, :, cols].astype(f32)
                    + gate[:, cols] * proj[tok * rows : (tok + 1) * rows]
                ).astype(bf16)
        for h in (j, 2 + j):
            cols = pl.ds(h * sub, sub)
            kept[h] = pltpu.make_async_copy(ob.at[h, 0], out_hbm.at[1, :, cols], local.at[10 + h])
            near[h] = copies.make(f"o{h}", ob.at[h, 1], ou.at[1, h], me.to(flip=True))
            next0[h] = copies.make(f"n{h}", ob.at[h, 0], ou.at[0, h], (after, me.head, 0))
            next1[h] = pltpu.make_async_remote_copy(
                src_ref=ob.at[h, 1], dst_ref=ou.at[0, h],
                send_sem=local.at[2 + h], recv_sem=recv.at[copies.count - 1],
                device_id=(after, me.head, 1), device_id_type=MESH,
            )

        @pl.when(core == 0)
        def _():
            for h in (j, 2 + j):
                near[h].start()
                kept[h].start()

        @pl.when(sends_on)
        def _():
            for h in (j, 2 + j):
                next0[h].start()
                next1[h].start()

    def keep(slot, h):
        cols = pl.ds(h * sub, sub)
        return pltpu.make_async_copy(
            ou.at[slot, h], out_hbm.at[slot, :, cols], local.at[14 + 4 * slot + h]
        )

    @pl.when(core == 1)
    def _():
        for h in range(4):
            near[h].wait_recv()
            keep(1, h).start()

    @pl.when(frame > 0)
    def _():
        for h in range(4):
            next0[h].wait_recv()
            keep(0, h).start()

    @pl.when(core == 0)
    def _():
        for h in range(4):
            near[h].wait_send()
            kept[h].wait()

    @pl.when(core == 1)
    def _():
        for h in range(4):
            keep(1, h).wait()

    @pl.when(frame > 0)
    def _():
        for h in range(4):
            keep(0, h).wait()

    @pl.when(frame == 0)
    def _():
        noise_copy.wait()

    @pl.when(sends_on)
    def _():
        for h in range(4):
            next0[h].wait_send()
            next1[h].wait_send()

    @pl.when(has_beside)
    def _():
        for n in names:
            copies.all["kv" + n].wait_send()

    copies.sent(skip=[f"{t}{h}" for t in "on" for h in range(4)] + ["kv" + n for n in names])


def body(queue, timesteps, mod_table, w_qkv, norm_gains, w_out, noise_frame):
    slots, rows, width = queue.shape
    hs = w_out.shape[1]
    bf16, f32 = jnp.bfloat16, jnp.float32
    hbm = pl.BlockSpec(memory_space=pl.ANY)
    smem = pl.BlockSpec(memory_space=pltpu.SMEM)
    tokens = NZ * rows
    keys = NX * 2 * tokens
    eighth = width // 8
    half = width // 2
    sub = half // 2
    table = jnp.transpose(mod_table, (1, 0, 2))
    return pl.pallas_call(
        block_kernel,
        out_shape=jax.ShapeDtypeStruct(queue.shape, bf16),
        in_specs=[smem] + [hbm] * 6,
        out_specs=hbm,
        scratch_shapes=[
            pltpu.VMEM(table.shape, f32),
            pltpu.VMEM(queue.shape, bf16),
            pltpu.VMEM(norm_gains.shape, f32),
            pltpu.VMEM((NZ, 2 * rows, width), bf16),
            pltpu.VMEM((NX, 8, eighth, 3 * hs), bf16),
            pltpu.VMEM((NX, 2, NZ, rows, 2 * hs), bf16),
            pltpu.VMEM((NX * 2, NZ, rows, 2 * hs), bf16),
            pltpu.VMEM((NX, 2, NZ, rows, hs), bf16),
            pltpu.VMEM((NX * 2, NZ, rows, hs), bf16),
            pltpu.VMEM((2, NX * 2, NZ, rows, 2 * hs), bf16),
            pltpu.VMEM((3, hs, keys), bf16),
            pltpu.VMEM((3, keys, 2 * hs), bf16),
            pltpu.VMEM((NX, 2 * tokens, 2 * hs), f32),
            pltpu.VMEM((NX, 2 * tokens, hs), f32),
            pltpu.VMEM((NX, NZ, 2 * rows, hs), bf16),
            pltpu.VMEM((NX, NZ, 2 * rows, hs), bf16),
            pltpu.VMEM((NZ, 8, hs // 8, width), bf16),
            pltpu.VMEM((4, 2 * rows, sub), bf16),
            pltpu.VMEM((4, 2 * rows, sub), bf16),
            pltpu.VMEM((4, 2 * rows, sub), bf16),
            pltpu.VMEM((2, 2 * rows, sub), bf16),
            pltpu.VMEM((2, 2 * rows, sub), bf16),
            pltpu.VMEM((4, 2 * rows, sub), bf16),
            pltpu.VMEM((4, 2 * rows, sub), bf16),
            pltpu.VMEM((2, rows, width), bf16),
            pltpu.VMEM((4, 2, rows, sub), bf16),
            pltpu.VMEM((2, 4, rows, sub), bf16),
            pltpu.SemaphoreType.DMA((22,)),
            pltpu.SemaphoreType.DMA((200,)),
            pltpu.SemaphoreType.DMA((200,)),
        ],
        compiler_params=pltpu.CompilerParams(
            collective_id=0, has_side_effects=True, vmem_limit_bytes=56 * 1024 * 1024
        ),
        name="block",
    )(
        timesteps, table, queue, noise_frame, norm_gains,
        w_qkv.reshape(8, eighth, 3 * hs), w_out.reshape(8, hs // 8, width),
    )


def solution(mesh):
    return jax.shard_map(
        body,
        mesh=mesh,
        in_specs=(
            P("frame", ("head", "tok"), None),
            P("frame"),
            P(),
            P(None, "head", None),
            P(),
            P("head", None, None),
            P(("head", "tok"), None),
        ),
        out_specs=P("frame", ("head", "tok"), None),
        check_vma=False,
    )
```

```python
import functools

import jax
import jax.numpy as jnp
from jax import lax
from jax.experimental import pallas as pl
from jax.experimental.pallas import tpu as pltpu
from jax.sharding import PartitionSpec as P

MESH = pl.DeviceIdType.MESH
NX = 4
NY = 4
NZ = 4
OWN, LEFT, RIGHT, OPP = 0, 1, 2, 3


class Place:
    def __init__(self):
        self.frame = lax.axis_index("frame")
        self.head = lax.axis_index("head")
        self.core = lax.axis_index("tok")
        self.x, self.zh = self.head // NZ, self.head % NZ
        self.y, self.zl = self.frame // 2, self.frame % 2

    def to(self, x=0, z=0, y=0, frame=0, flip=False, core=None):
        head = ((self.x + x) % NX) * NZ + (self.zh + z) % NZ
        own = ((self.y + y) % NY) * 2 + self.zl if frame == 0 else self.frame + frame
        tok = self.core if core is None else core
        tok = 1 - tok if flip else tok
        return (own, head, tok)


class Copies:
    def __init__(self, send, recv):
        self.send, self.recv, self.count, self.all = send, recv, 0, {}

    def make(self, name, src, dst, device):
        k = self.count
        self.count += 1
        copy = pltpu.make_async_remote_copy(
            src_ref=src,
            dst_ref=dst,
            send_sem=self.send.at[k],
            recv_sem=self.recv.at[k],
            device_id=device,
            device_id_type=MESH,
        )
        self.all[name] = copy
        return copy

    def start(self, name, src, dst, device):
        self.make(name, src, dst, device).start()

    def got(self, *names):
        for name in names:
            self.all[name].wait_recv()

    def sent(self, skip=()):
        for name, copy in self.all.items():
            if name not in skip:
                copy.wait_send()


def greet(devices, count):
    barrier = pltpu.get_barrier_semaphore()
    for device in devices:
        pl.semaphore_signal(barrier, inc=1, device_id=device, device_id_type=MESH)
    pl.semaphore_wait(barrier, count)


class Gather:
    def __init__(self, tag, copies, me, ring, source, held, half, whole):
        self.tag, self.copies, self.me, self.ring = tag, copies, me, ring
        self.source, self.held, self.half, self.whole = source, held, half, whole
        self.mine = me.core * NY + me.y
        self.left = me.core * NY + (me.y + NY - 1) % NY
        self.right = me.core * NY + (me.y + 1) % NY
        self.far = me.core * NY + (me.y + 2) % NY

    def part(self, rel, eighth, which):
        return self.half(self.held, rel, eighth, which)

    def go(self, name, src, dst, device):
        self.copies.start(self.tag + name, src, dst, device)

    def got(self, *names):
        self.copies.got(*[self.tag + name for name in names])

    def ring_start(self):
        e = self.mine
        self.go("r", self.source(e), self.whole(self.held, LEFT, e), self.me.to(**{self.ring: 1}))
        self.go("l", self.source(e), self.whole(self.held, RIGHT, e), self.me.to(**{self.ring: -1}))

    def ring_relay(self):
        e = self.mine
        self.got("r")
        self.go("rr", self.part(LEFT, e, 0), self.part(OPP, e, 0), self.me.to(**{self.ring: 1}))
        self.y_start(LEFT)
        self.got("l")
        self.go("ll", self.part(RIGHT, e, 1), self.part(OPP, e, 1), self.me.to(**{self.ring: -1}))
        self.y_start(RIGHT)

    def ring_end(self):
        self.got("rr", "ll")
        self.y_start(OPP)

    def y_start(self, rel):
        n, e = str(rel), self.mine
        self.go("yr" + n, self.whole(self.held, rel, e), self.whole(self.held, rel, e), self.me.to(y=1))
        self.go("yl" + n, self.whole(self.held, rel, e), self.whole(self.held, rel, e), self.me.to(y=-1))
        self.go("s0" + n, self.whole(self.held, rel, e), self.whole(self.held, rel, e), self.me.to(flip=True))

    def y_relay(self, rel):
        n = str(rel)
        self.got("yr" + n)
        e = self.left
        self.go("yrr" + n, self.part(rel, e, 0), self.part(rel, e, 0), self.me.to(y=1))
        self.go("s1" + n, self.whole(self.held, rel, e), self.whole(self.held, rel, e), self.me.to(flip=True))
        self.got("yl" + n)
        e = self.right
        self.go("yll" + n, self.part(rel, e, 1), self.part(rel, e, 1), self.me.to(y=-1))
        self.go("s2" + n, self.whole(self.held, rel, e), self.whole(self.held, rel, e), self.me.to(flip=True))

    def y_end(self, rel):
        n = str(rel)
        self.got("yrr" + n, "yll" + n)
        e = self.far
        self.go("s3" + n, self.whole(self.held, rel, e), self.whole(self.held, rel, e), self.me.to(flip=True))

    def done(self, rel):
        n = str(rel)
        self.got("s0" + n, "s1" + n, "s2" + n, "s3" + n)


class PairGather(Gather):
    def __init__(self, *args):
        super().__init__(*args)
        me = self.me
        twin = me.y * 2 + 1 - me.zl
        step = 2 * me.zl - 1
        self.twin = (twin, me.head, me.core)
        self.hop = (twin, me.x * NZ + (me.zh + step + NZ) % NZ, me.core)
        self.got_first, self.got_second = 1 + me.zl, 2 - me.zl

    def ring_start(self):
        e = self.mine
        self.go("r", self.source(e), self.whole(self.held, self.got_second, e), self.hop)

    def ring_relay(self):
        self.got("r")
        part = self.whole(self.held, self.got_first, self.mine)
        self.go("x", part, part, self.twin)

    def ring_last(self):
        e = self.mine
        self.got("x")
        self.go("rr", self.whole(self.held, self.got_second, e), self.whole(self.held, OPP, e), self.hop)
        self.y_start(LEFT)
        self.y_start(RIGHT)

    def ring_end(self):
        self.got("rr")
        self.y_start(OPP)


class Direct:
    def __init__(self, tag, copies, me, source, held, count, cols):
        self.tag, self.copies, self.me, self.count, self.cols = tag, copies, me, count, cols
        self.source, self.held = source, held
        self.quad = pl.ds(me.core * NY, NY)
        self.low = count // 2

    def rows(self, rel, first, count):
        return self.held.at[rel, self.quad, pl.ds(first, count), self.cols]

    def go(self, name, src, dst, device):
        self.copies.start(self.tag + name, src, dst, device)

    def got(self, *names):
        self.copies.got(*[self.tag + name for name in names])

    def start(self):
        source = self.source.at[self.quad, pl.ds(0, self.count), self.cols]
        self.go("r", source, self.rows(LEFT, 0, self.count), self.me.to(x=1))
        self.go("l", source, self.rows(RIGHT, 0, self.count), self.me.to(x=-1))

    def beside(self, rel):
        part = self.rows(rel, 0, self.count)
        self.go("s" + str(rel), part, part, self.me.to(flip=True))

    def relay(self):
        low, high = self.low, self.count - self.low
        self.got("r")
        self.go("rr", self.rows(LEFT, 0, low), self.rows(OPP, 0, low), self.me.to(x=1))
        self.beside(LEFT)
        self.got("l")
        self.go("ll", self.rows(RIGHT, low, high), self.rows(OPP, low, high), self.me.to(x=-1))
        self.beside(RIGHT)

    def end(self):
        self.got("rr", "ll")
        self.beside(OPP)


def rms_scale(values, gain):
    return values * lax.rsqrt(jnp.mean(values * values, axis=-1, keepdims=True) + 1e-06) * gain


def block_kernel(
    steps_ref, mod_hbm, queue_hbm, noise_hbm, gains_hbm, w_hbm, wo_hbm, out_hbm,
    mod, queue_ref, gains_ref, xg, wg, sbk, rbk, sbq, rbq, kvb, kt, vx, oa, top, attn_s, attn_g, wo, po, pr_s, pl_s, rl, rr, fl, fr,
    qb, ob, ou, local, send, recv,
):
    me = Place()
    core, frame = me.core, me.frame
    frames = lax.axis_size("frame")
    rows, width = queue_ref.shape[1:]
    hs = gains_ref.shape[1]
    bf16, f32 = jnp.bfloat16, jnp.float32
    half = width // 2
    tokens = NZ * rows
    keys = NX * 2 * tokens
    beside = frame + 2 * core - 1
    has_beside = jnp.logical_and(beside >= 0, beside < frames)
    after = (frame + 1) % frames
    before = (frame + frames - 1) % frames
    back = {LEFT: RIGHT, RIGHT: LEFT, OPP: OPP}
    shift = {LEFT: -1, RIGHT: 1, OPP: 2}

    mod_copy = pltpu.make_async_copy(mod_hbm, mod, local.at[6])
    mod_copy.start()
    queue_copy = pltpu.make_async_copy(queue_hbm, queue_ref, local.at[7])
    queue_copy.start()
    gains_copy = pltpu.make_async_copy(gains_hbm, gains_ref, local.at[8])
    gains_copy.start()
    copies = Copies(send, recv)
    outs = PairGather(
        "o", copies, me, "z", (lambda e: wo_hbm.at[e]), wo,
        lambda ref, rel, e, which: ref.at[rel, e, :, pl.ds(which * half, half)],
        lambda ref, rel, e: ref.at[rel, e],
    )
    partners = [me.to(flip=True)]
    for step in (1, -1, 2):
        partners += [me.to(x=step), me.to(x=step, flip=True), me.to(z=step)]
    partners += [me.to(y=1), me.to(y=-1)]
    partners += [(before, me.head, 1), outs.twin, outs.hop]
    barrier = pltpu.get_barrier_semaphore()
    for device in partners:
        pl.semaphore_signal(barrier, inc=1, device_id=device, device_id_type=MESH)

    @pl.when(core == 1)
    def _():
        for tok in range(2):
            pl.semaphore_signal(
                barrier, inc=1, device_id=(after, me.head, tok), device_id_type=MESH
            )

    queue_copy.wait()
    mod_copy.wait()
    for slot in range(2):
        level = pl.ds(steps_ref[slot], 1)
        x = queue_ref[slot].astype(f32)
        centred = x - jnp.mean(x, axis=-1, keepdims=True)
        normed = centred * lax.rsqrt(jnp.mean(centred * centred, axis=-1, keepdims=True) + 1e-06)
        xg[OWN, slot * rows : (slot + 1) * rows, :] = (
            normed * (1.0 + mod[1, level, :]) + mod[0, level, :]
        ).astype(bf16)
    pl.semaphore_wait(barrier, len(partners) + 2 * core)

    rows_in = wg.shape[2]

    q_cols, kv_cols = pl.ds(0, hs), pl.ds(hs, 2 * hs)

    def gather(tag, cols, direct):
        part = (rows_in - direct) // 2
        ringed = Gather(
            "w" + tag, copies, me, "x",
            (lambda e: w_hbm.at[e, pl.ds(direct, 2 * part), cols]), wg,
            lambda ref, rel, e, which: ref.at[rel, e, pl.ds(direct + which * part, part), cols],
            lambda ref, rel, e: ref.at[rel, e, pl.ds(direct, 2 * part), cols],
        )
        return ringed, Direct("d" + tag, copies, me, w_hbm, wg, direct, cols)

    wk, dk = gather("k", kv_cols, rows_in * 5 // 12)
    wq, dq = gather("q", q_cols, rows_in // 2)
    wk.ring_start()
    own_w = pltpu.make_async_copy(w_hbm, wg.at[OWN], local.at[0])
    own_w.start()
    own_wo = pltpu.make_async_copy(wo_hbm, wo.at[OWN], local.at[1])
    own_wo.start()
    first, second = pl.ds(0, rows), pl.ds(rows, rows)
    copies.start("zr0", xg.at[OWN, first], xg.at[LEFT, first], me.to(z=1))
    copies.start("zl1", xg.at[OWN, second], xg.at[RIGHT, second], me.to(z=-1))
    copies.start("zr1", xg.at[OWN, second], xg.at[LEFT, second], me.to(z=1))
    copies.start("zl0", xg.at[OWN, first], xg.at[RIGHT, first], me.to(z=-1))
    copies.start("qs", queue_hbm.at[1 - core], qb.at[core], me.to(flip=True))

    wk.ring_relay()
    dk.start()
    wq.ring_start()
    copies.got("zr0")
    copies.start("zrr", xg.at[LEFT, first], xg.at[OPP, first], me.to(z=1))
    copies.got("zl1")
    copies.start("zll", xg.at[RIGHT, second], xg.at[OPP, second], me.to(z=-1))
    outs.ring_start()
    wk.ring_end()
    wk.y_relay(LEFT)
    wk.y_relay(RIGHT)
    dk.relay()
    wq.ring_relay()
    dq.start()
    wk.y_relay(OPP)
    wk.y_end(LEFT)
    wk.y_end(RIGHT)
    dk.end()
    gains_copy.wait()
    q_gain = gains_ref[0:1, :] * f32(1.4426950408889634 / hs**0.5)
    k_gain = gains_ref[1:2, :]
    groups = (pl.ds(0, NZ - 1), pl.ds(NZ - 1, 1))
    sizes = (NZ - 1, 1)

    def send_rows(tag, sent, home, rel, which):
        if rel == OWN:
            copies.start(
                "a" + tag, sent.at[OWN, 1 - core, which], home.at[core, which], me.to(flip=True)
            )
            home[core, which] = sent[OWN, core, which]
            return
        spot = home.at[back[rel] * 2 + core, which]
        copies.start("a" + tag, sent.at[rel, core, which], spot, me.to(x=shift[rel]))
        copies.start(
            "b" + tag, sent.at[rel, 1 - core, which], spot, me.to(x=shift[rel], flip=True)
        )

    def project_kv(rel, group):
        which, count = groups[group], sizes[group]
        xs = xg[which].reshape(count * 2 * rows, width)
        w = wg[rel, :, :, hs:].reshape(width, 2 * hs)
        kv = jnp.dot(xs, w, preferred_element_type=f32)
        k = rms_scale(kv[:, :hs], k_gain)
        out = jnp.concatenate([k, kv[:, hs:]], axis=-1).astype(bf16)
        out = out.reshape(count, 2, rows, 2 * hs)
        for slot in range(2):
            sbk[rel, slot, which] = out[:, slot]
        send_rows(f"k{rel}{group}", sbk, rbk, rel, which)

    def project_q(rel):
        xs = xg[...].reshape(NZ * 2 * rows, width)
        w = wg[rel, :, :, :hs].reshape(width, hs)
        q = rms_scale(jnp.dot(xs, w, preferred_element_type=f32), q_gain)
        out = q.astype(bf16).reshape(NZ, 2, rows, hs)
        for slot in range(2):
            sbq[rel, slot] = out[:, slot]
        send_rows(f"q{rel}", sbq, rbq, rel, pl.ds(0, NZ))

    def share(rel, group):
        n = f"{rel}{group}"
        copies.got("ak" + n)
        if rel != OWN:
            copies.got("bk" + n)
        spot = OWN if rel == OWN else back[rel]
        pair = pl.ds(spot * 2, 2)
        src = rbk.at[pair, groups[group]]
        side = copies.make("kv" + n, src, kvb.at[1, pair, groups[group]], (beside, me.head, 1 - core))

        @pl.when(has_beside)
        def _():
            side.start()

        copies.start("ks" + n, src, kvb.at[0, pair, groups[group]], me.to(flip=True))

    own_w.wait()
    copies.got("zr1", "zl0")
    project_kv(OWN, 0)
    wq.ring_end()
    wk.done(LEFT)
    dk.got("s1")
    project_kv(LEFT, 0)
    wk.done(RIGHT)
    dk.got("s2")
    project_kv(RIGHT, 0)
    outs.ring_relay()
    share(OWN, 0)
    wk.y_end(OPP)
    wq.y_relay(LEFT)
    dq.relay()
    wk.done(OPP)
    dk.got("s3")
    project_kv(OPP, 0)
    wq.y_relay(RIGHT)
    share(LEFT, 0)
    share(RIGHT, 0)
    wq.y_relay(OPP)
    wq.y_end(LEFT)
    copies.got("zrr", "zll")
    for rel in (OPP, LEFT, RIGHT, OWN):
        project_kv(rel, 1)
    share(OPP, 0)
    outs.ring_last()
    dq.end()
    wq.y_end(RIGHT)
    wq.y_end(OPP)
    project_q(OWN)
    wq.done(LEFT)
    dq.got("s1")
    project_q(LEFT)
    share(LEFT, 1)
    wq.done(RIGHT)
    dq.got("s2")
    project_q(RIGHT)
    share(OPP, 1)
    share(RIGHT, 1)
    share(OWN, 1)
    wq.done(OPP)
    dq.got("s3")
    project_q(OPP)
    outs.ring_end()
    names = [f"{rel}{group}" for rel in range(4) for group in range(2)]

    ones = jnp.ones((keys, hs), bf16)

    def take(which, kv):
        kt[which] = kv[:, :hs].T
        vx[which, :, :hs] = kv[:, hs:]
        vx[which, :, hs:] = ones

    block = 2 * tokens

    def queries(i):
        return rbq[pl.ds(2 * i, 2)].reshape(block, hs)

    def first_part(rx):
        q = queries(rx)
        scores = [jnp.dot(q, kt[j], preferred_element_type=f32) for j in range(2)]
        peak = jnp.maximum(
            jnp.max(scores[0], axis=-1, keepdims=True), jnp.max(scores[1], axis=-1, keepdims=True)
        )
        total = jnp.zeros((block, 2 * hs), f32)
        for j in range(2):
            p = jnp.exp2(scores[j] - peak).astype(bf16)
            total += jnp.dot(p, vx[j], preferred_element_type=f32)
        oa[rx] = total
        top[rx] = jnp.broadcast_to(peak, (block, hs))

    def attend(rx):
        @pl.when(has_beside)
        def _():
            s = jnp.dot(queries(rx), kt[2], preferred_element_type=f32)
            old = top[rx][:, :1]
            peak = jnp.maximum(old, jnp.max(s, axis=-1, keepdims=True))
            p = jnp.exp2(s - peak).astype(bf16)
            oa[rx] = oa[rx] * jnp.exp2(old - peak) + jnp.dot(
                p, vx[2], preferred_element_type=f32
            )

        o = oa[rx]
        attn = (o[:, :hs] / o[:, hs:]).astype(bf16).reshape(2, NZ, rows, hs)
        attn_g[rx, OWN] = attn[:, OWN].reshape(2 * rows, hs)
        for rz in (LEFT, RIGHT, OPP):
            attn_s[rx, rz] = attn[:, rz].reshape(2 * rows, hs)
            copies.start(
                f"t{rx}{rz}", attn_s.at[rx, rz], attn_g.at[rx, back[rz]], me.to(z=shift[rz])
            )

    def contribution(rx):
        copies.got(*[f"t{rx}{rz}" for rz in (LEFT, RIGHT, OPP)])
        a = jnp.concatenate([attn_g[rx, rz] for rz in range(NZ)], axis=-1)
        return jnp.dot(a, wo[...].reshape(NZ * hs, width), preferred_element_type=f32)

    take(0, rbk[...].reshape(keys, 2 * hs))
    copies.got(*["ks" + n for n in names])
    take(1, kvb[0].reshape(keys, 2 * hs))
    copies.got("aq0")
    for rel in (LEFT, RIGHT, OPP):
        copies.got(f"aq{rel}", f"bq{rel}")
    first_part(OPP)
    outs.y_relay(LEFT)
    outs.y_relay(RIGHT)
    first_part(RIGHT)
    outs.y_relay(OPP)

    @pl.when(has_beside)
    def _():
        for n in names:
            copies.got("kv" + n)
        take(2, kvb[1].reshape(keys, 2 * hs))

    attend(OPP)
    attend(RIGHT)
    for rel in (LEFT, RIGHT, OPP):
        outs.y_end(rel)
    first_part(LEFT)
    attend(LEFT)
    own_wo.wait()
    for rel in (LEFT, RIGHT, OPP):
        outs.done(rel)

    sub = half // 2
    p = contribution(OPP).astype(bf16)
    for j in range(2):
        po[j] = p[:, j * sub : (j + 1) * sub]
        po[2 + j] = p[:, half + j * sub : half + (j + 1) * sub]
        copies.start(f"rl{j}", po.at[j], rl.at[j], me.to(x=1))
        copies.start(f"rr{j}", po.at[2 + j], rr.at[j], me.to(x=-1))
    first_part(OWN)
    attend(OWN)

    right = contribution(RIGHT)
    for j in range(2):
        pr_s[2 + j] = right[:, half + j * sub : half + (j + 1) * sub].astype(bf16)
        copies.start(f"fl{2 + j}", pr_s.at[2 + j], fl.at[2 + j], me.to(x=1))
    left = contribution(LEFT)
    for j in range(2):
        pl_s[j] = left[:, j * sub : (j + 1) * sub].astype(bf16)
        copies.start(f"fr{j}", pl_s.at[j], fr.at[j], me.to(x=-1))
    for j in range(2):
        copies.got(f"rl{j}")
        pr_s[j] = (right[:, j * sub : (j + 1) * sub] + rl[j].astype(f32)).astype(bf16)
        copies.start(f"fl{j}", pr_s.at[j], fl.at[j], me.to(x=1))
        copies.got(f"rr{j}")
        pl_s[2 + j] = (
            left[:, half + j * sub : half + (j + 1) * sub] + rr[j].astype(f32)
        ).astype(bf16)
        copies.start(f"fr{2 + j}", pl_s.at[2 + j], fr.at[2 + j], me.to(x=-1))

    p = contribution(OWN)
    copies.got("qs")
    qb[core] = queue_ref[core]
    gate = mod[2, pl.ds(steps_ref[core], 1), :]
    sends_on = jnp.logical_and(core == 1, frame < frames - 1)
    near, next0, next1, kept = {}, {}, {}, {}
    noise_copy = pltpu.make_async_copy(noise_hbm, out_hbm.at[0], local.at[9])

    @pl.when(frame == 0)
    def _():
        noise_copy.start()

    for j in range(2):
        copies.got(f"fl{j}", f"fr{j}", f"fl{2 + j}", f"fr{2 + j}")
        for h in (j, 2 + j):
            cols = slice(h * sub, (h + 1) * sub)
            proj = p[:, cols] + fl[h].astype(f32) + fr[h].astype(f32)
            for tok in range(2):
                ob[h, tok] = (
                    qb[tok, :, cols].astype(f32)
                    + gate[:, cols] * proj[tok * rows : (tok + 1) * rows]
                ).astype(bf16)
        for h in (j, 2 + j):
            cols = pl.ds(h * sub, sub)
            kept[h] = pltpu.make_async_copy(ob.at[h, 0], out_hbm.at[1, :, cols], local.at[10 + h])
            near[h] = copies.make(f"o{h}", ob.at[h, 1], ou.at[1, h], me.to(flip=True))
            next0[h] = copies.make(f"n{h}", ob.at[h, 0], ou.at[0, h], (after, me.head, 0))
            next1[h] = pltpu.make_async_remote_copy(
                src_ref=ob.at[h, 1], dst_ref=ou.at[0, h],
                send_sem=local.at[2 + h], recv_sem=recv.at[copies.count - 1],
                device_id=(after, me.head, 1), device_id_type=MESH,
            )

        @pl.when(core == 0)
        def _():
            for h in (j, 2 + j):
                near[h].start()
                kept[h].start()

        @pl.when(sends_on)
        def _():
            for h in (j, 2 + j):
                next0[h].start()
                next1[h].start()

    def keep(slot, h):
        cols = pl.ds(h * sub, sub)
        return pltpu.make_async_copy(
            ou.at[slot, h], out_hbm.at[slot, :, cols], local.at[14 + 4 * slot + h]
        )

    @pl.when(core == 1)
    def _():
        for h in range(4):
            near[h].wait_recv()
            keep(1, h).start()

    @pl.when(frame > 0)
    def _():
        for h in range(4):
            next0[h].wait_recv()
            keep(0, h).start()

    @pl.when(core == 0)
    def _():
        for h in range(4):
            near[h].wait_send()
            kept[h].wait()

    @pl.when(core == 1)
    def _():
        for h in range(4):
            keep(1, h).wait()

    @pl.when(frame > 0)
    def _():
        for h in range(4):
            keep(0, h).wait()

    @pl.when(frame == 0)
    def _():
        noise_copy.wait()

    @pl.when(sends_on)
    def _():
        for h in range(4):
            next0[h].wait_send()
            next1[h].wait_send()

    @pl.when(has_beside)
    def _():
        for n in names:
            copies.all["kv" + n].wait_send()

    copies.sent(skip=[f"{t}{h}" for t in "on" for h in range(4)] + ["kv" + n for n in names])


def body(queue, timesteps, mod_table, w_qkv, norm_gains, w_out, noise_frame):
    slots, rows, width = queue.shape
    hs = w_out.shape[1]
    bf16, f32 = jnp.bfloat16, jnp.float32
    hbm = pl.BlockSpec(memory_space=pl.ANY)
    smem = pl.BlockSpec(memory_space=pltpu.SMEM)
    tokens = NZ * rows
    keys = NX * 2 * tokens
    eighth = width // 8
    half = width // 2
    sub = half // 2
    table = jnp.transpose(mod_table, (1, 0, 2))
    return pl.pallas_call(
        block_kernel,
        out_shape=jax.ShapeDtypeStruct(queue.shape, bf16),
        in_specs=[smem] + [hbm] * 6,
        out_specs=hbm,
        scratch_shapes=[
            pltpu.VMEM(table.shape, f32),
            pltpu.VMEM(queue.shape, bf16),
            pltpu.VMEM(norm_gains.shape, f32),
            pltpu.VMEM((NZ, 2 * rows, width), bf16),
            pltpu.VMEM((NX, 8, eighth, 3 * hs), bf16),
            pltpu.VMEM((NX, 2, NZ, rows, 2 * hs), bf16),
            pltpu.VMEM((NX * 2, NZ, rows, 2 * hs), bf16),
            pltpu.VMEM((NX, 2, NZ, rows, hs), bf16),
            pltpu.VMEM((NX * 2, NZ, rows, hs), bf16),
            pltpu.VMEM((2, NX * 2, NZ, rows, 2 * hs), bf16),
            pltpu.VMEM((3, hs, keys), bf16),
            pltpu.VMEM((3, keys, 2 * hs), bf16),
            pltpu.VMEM((NX, 2 * tokens, 2 * hs), f32),
            pltpu.VMEM((NX, 2 * tokens, hs), f32),
            pltpu.VMEM((NX, NZ, 2 * rows, hs), bf16),
            pltpu.VMEM((NX, NZ, 2 * rows, hs), bf16),
            pltpu.VMEM((NZ, 8, hs // 8, width), bf16),
            pltpu.VMEM((4, 2 * rows, sub), bf16),
            pltpu.VMEM((4, 2 * rows, sub), bf16),
            pltpu.VMEM((4, 2 * rows, sub), bf16),
            pltpu.VMEM((2, 2 * rows, sub), bf16),
            pltpu.VMEM((2, 2 * rows, sub), bf16),
            pltpu.VMEM((4, 2 * rows, sub), bf16),
            pltpu.VMEM((4, 2 * rows, sub), bf16),
            pltpu.VMEM((2, rows, width), bf16),
            pltpu.VMEM((4, 2, rows, sub), bf16),
            pltpu.VMEM((2, 4, rows, sub), bf16),
            pltpu.SemaphoreType.DMA((22,)),
            pltpu.SemaphoreType.DMA((200,)),
            pltpu.SemaphoreType.DMA((200,)),
        ],
        compiler_params=pltpu.CompilerParams(
            collective_id=0, has_side_effects=True, vmem_limit_bytes=56 * 1024 * 1024
        ),
        name="block",
    )(
        timesteps, table, queue, noise_frame, norm_gains,
        w_qkv.reshape(8, eighth, 3 * hs), w_out.reshape(8, hs // 8, width),
    )


def solution(mesh):
    return jax.shard_map(
        body,
        mesh=mesh,
        in_specs=(
            P("frame", ("head", "tok"), None),
            P("frame"),
            P(),
            P(None, "head", None),
            P(),
            P("head", None, None),
            P(("head", "tok"), None),
        ),
        out_specs=P("frame", ("head", "tok"), None),
        check_vma=False,
    )
```

```python
import functools

import jax
import jax.numpy as jnp
from jax import lax
from jax.experimental import pallas as pl
from jax.experimental.pallas import tpu as pltpu
from jax.sharding import PartitionSpec as P

MESH = pl.DeviceIdType.MESH
NX = 4
NY = 4
NZ = 4
PIECES = 4
OWN, LEFT, RIGHT, OPP = 0, 1, 2, 3


class Place:
    def __init__(self):
        self.frame = lax.axis_index("frame")
        self.head = lax.axis_index("head")
        self.core = lax.axis_index("tok")
        self.x, self.zh = self.head // NZ, self.head % NZ
        self.y, self.zl = self.frame // 2, self.frame % 2

    def to(self, x=0, z=0, y=0, frame=0, flip=False, core=None):
        head = ((self.x + x) % NX) * NZ + (self.zh + z) % NZ
        own = ((self.y + y) % NY) * 2 + self.zl if frame == 0 else self.frame + frame
        tok = self.core if core is None else core
        tok = 1 - tok if flip else tok
        return (own, head, tok)


class Copies:
    def __init__(self, send, recv):
        self.send, self.recv, self.count, self.all = send, recv, 0, {}

    def make(self, name, src, dst, device):
        k = self.count
        self.count += 1
        copy = pltpu.make_async_remote_copy(
            src_ref=src,
            dst_ref=dst,
            send_sem=self.send.at[k],
            recv_sem=self.recv.at[k],
            device_id=device,
            device_id_type=MESH,
        )
        self.all[name] = copy
        return copy

    def start(self, name, src, dst, device):
        self.make(name, src, dst, device).start()

    def got(self, *names):
        for name in names:
            self.all[name].wait_recv()

    def sent(self, skip=()):
        for name, copy in self.all.items():
            if name not in skip:
                copy.wait_send()


def greet(devices, count):
    barrier = pltpu.get_barrier_semaphore()
    for device in devices:
        pl.semaphore_signal(barrier, inc=1, device_id=device, device_id_type=MESH)
    pl.semaphore_wait(barrier, count)


class Gather:
    def __init__(self, tag, copies, me, ring, source, held, half, whole):
        self.tag, self.copies, self.me, self.ring = tag, copies, me, ring
        self.source, self.held, self.half, self.whole = source, held, half, whole
        self.mine = me.core * NY + me.y
        self.left = me.core * NY + (me.y + NY - 1) % NY
        self.right = me.core * NY + (me.y + 1) % NY
        self.far = me.core * NY + (me.y + 2) % NY

    def part(self, rel, eighth, which):
        return self.half(self.held, rel, eighth, which)

    def go(self, name, src, dst, device):
        self.copies.start(self.tag + name, src, dst, device)

    def got(self, *names):
        self.copies.got(*[self.tag + name for name in names])

    def ring_start(self):
        e = self.mine
        self.go("r", self.source(e), self.whole(self.held, LEFT, e), self.me.to(**{self.ring: 1}))
        self.go("l", self.source(e), self.whole(self.held, RIGHT, e), self.me.to(**{self.ring: -1}))

    def ring_relay(self):
        e = self.mine
        self.got("r")
        self.go("rr", self.part(LEFT, e, 0), self.part(OPP, e, 0), self.me.to(**{self.ring: 1}))
        self.y_start(LEFT)
        self.got("l")
        self.go("ll", self.part(RIGHT, e, 1), self.part(OPP, e, 1), self.me.to(**{self.ring: -1}))
        self.y_start(RIGHT)

    def ring_end(self):
        self.got("rr", "ll")
        self.y_start(OPP)

    def y_start(self, rel):
        n, e = str(rel), self.mine
        self.go("yr" + n, self.whole(self.held, rel, e), self.whole(self.held, rel, e), self.me.to(y=1))
        self.go("yl" + n, self.whole(self.held, rel, e), self.whole(self.held, rel, e), self.me.to(y=-1))
        self.go("s0" + n, self.whole(self.held, rel, e), self.whole(self.held, rel, e), self.me.to(flip=True))

    def y_relay(self, rel):
        n = str(rel)
        self.got("yr" + n)
        e = self.left
        self.go("yrr" + n, self.part(rel, e, 0), self.part(rel, e, 0), self.me.to(y=1))
        self.go("s1" + n, self.whole(self.held, rel, e), self.whole(self.held, rel, e), self.me.to(flip=True))
        self.got("yl" + n)
        e = self.right
        self.go("yll" + n, self.part(rel, e, 1), self.part(rel, e, 1), self.me.to(y=-1))
        self.go("s2" + n, self.whole(self.held, rel, e), self.whole(self.held, rel, e), self.me.to(flip=True))

    def y_end(self, rel):
        n = str(rel)
        self.got("yrr" + n, "yll" + n)
        e = self.far
        self.go("s3" + n, self.whole(self.held, rel, e), self.whole(self.held, rel, e), self.me.to(flip=True))

    def done(self, rel):
        n = str(rel)
        self.got("s0" + n, "s1" + n, "s2" + n, "s3" + n)


class PairGather(Gather):
    def __init__(self, *args):
        super().__init__(*args)
        me = self.me
        twin = me.y * 2 + 1 - me.zl
        step = 2 * me.zl - 1
        self.twin = (twin, me.head, me.core)
        self.hop = (twin, me.x * NZ + (me.zh + step + NZ) % NZ, me.core)
        self.got_first, self.got_second = 1 + me.zl, 2 - me.zl

    def ring_start(self):
        e = self.mine
        self.go("r", self.source(e), self.whole(self.held, self.got_second, e), self.hop)

    def ring_relay(self):
        self.got("r")
        part = self.whole(self.held, self.got_first, self.mine)
        self.go("x", part, part, self.twin)

    def ring_last(self):
        e = self.mine
        self.got("x")
        self.go("rr", self.whole(self.held, self.got_second, e), self.whole(self.held, OPP, e), self.hop)
        self.y_start(LEFT)
        self.y_start(RIGHT)

    def ring_end(self):
        self.got("rr")
        self.y_start(OPP)


class Direct:
    def __init__(self, tag, copies, me, source, held, count, cols):
        self.tag, self.copies, self.me, self.count, self.cols = tag, copies, me, count, cols
        self.source, self.held = source, held
        self.quad = pl.ds(me.core * NY, NY)
        self.low = count // 2

    def rows(self, rel, first, count):
        return self.held.at[rel, self.quad, pl.ds(first, count), self.cols]

    def go(self, name, src, dst, device):
        self.copies.start(self.tag + name, src, dst, device)

    def got(self, *names):
        self.copies.got(*[self.tag + name for name in names])

    def start(self):
        source = self.source.at[self.quad, pl.ds(0, self.count), self.cols]
        self.go("r", source, self.rows(LEFT, 0, self.count), self.me.to(x=1))
        self.go("l", source, self.rows(RIGHT, 0, self.count), self.me.to(x=-1))

    def beside(self, rel):
        part = self.rows(rel, 0, self.count)
        self.go("s" + str(rel), part, part, self.me.to(flip=True))

    def relay(self):
        low, high = self.low, self.count - self.low
        self.got("r")
        self.go("rr", self.rows(LEFT, 0, low), self.rows(OPP, 0, low), self.me.to(x=1))
        self.beside(LEFT)
        self.got("l")
        self.go("ll", self.rows(RIGHT, low, high), self.rows(OPP, low, high), self.me.to(x=-1))
        self.beside(RIGHT)

    def end(self):
        self.got("rr", "ll")
        self.beside(OPP)


def rms_scale(values, gain):
    return values * lax.rsqrt(jnp.mean(values * values, axis=-1, keepdims=True) + 1e-06) * gain


def block_kernel(
    steps_ref, mod_hbm, queue_hbm, noise_hbm, gains_hbm, w_hbm, wo_hbm, out_hbm,
    mod, queue_ref, gains_ref, xg, wg, sbk, rbk, sbq, rbq, kvb, kt, vx, oa, top, attn_s, attn_g, wo, po, pr_s, pl_s, rl, rr, fl, fr,
    qb, ob, ou, local, send, recv,
):
    me = Place()
    core, frame = me.core, me.frame
    frames = lax.axis_size("frame")
    rows, width = queue_ref.shape[1:]
    hs = gains_ref.shape[1]
    bf16, f32 = jnp.bfloat16, jnp.float32
    half = width // 2
    tokens = NZ * rows
    keys = NX * 2 * tokens
    beside = frame + 2 * core - 1
    has_beside = jnp.logical_and(beside >= 0, beside < frames)
    after = (frame + 1) % frames
    before = (frame + frames - 1) % frames
    back = {LEFT: RIGHT, RIGHT: LEFT, OPP: OPP}
    shift = {LEFT: -1, RIGHT: 1, OPP: 2}

    norm_part, gate_part = pl.ds(0, 2), pl.ds(2, 1)
    mod_copy = pltpu.make_async_copy(mod_hbm.at[norm_part], mod.at[norm_part], local.at[6])
    mod_copy.start()
    queue_copy = pltpu.make_async_copy(queue_hbm, queue_ref, local.at[7])
    queue_copy.start()
    gains_copy = pltpu.make_async_copy(gains_hbm, gains_ref, local.at[8])
    gains_copy.start()
    copies = Copies(send, recv)
    outs = PairGather(
        "o", copies, me, "z", (lambda e: wo_hbm.at[e]), wo,
        lambda ref, rel, e, which: ref.at[rel, e, :, pl.ds(which * half, half)],
        lambda ref, rel, e: ref.at[rel, e],
    )
    partners = [me.to(flip=True)]
    for step in (1, -1, 2):
        partners += [me.to(x=step), me.to(x=step, flip=True), me.to(z=step)]
    partners += [me.to(y=1), me.to(y=-1)]
    partners += [(before, me.head, 1), outs.twin, outs.hop]
    barrier = pltpu.get_barrier_semaphore()
    for device in partners:
        pl.semaphore_signal(barrier, inc=1, device_id=device, device_id_type=MESH)

    @pl.when(core == 1)
    def _():
        for tok in range(2):
            pl.semaphore_signal(
                barrier, inc=1, device_id=(after, me.head, tok), device_id_type=MESH
            )

    queue_copy.wait()
    mod_copy.wait()
    for slot in range(2):
        level = pl.ds(steps_ref[slot], 1)
        x = queue_ref[slot].astype(f32)
        centred = x - jnp.mean(x, axis=-1, keepdims=True)
        normed = centred * lax.rsqrt(jnp.mean(centred * centred, axis=-1, keepdims=True) + 1e-06)
        xg[OWN, slot * rows : (slot + 1) * rows, :] = (
            normed * (1.0 + mod[1, level, :]) + mod[0, level, :]
        ).astype(bf16)
    pl.semaphore_wait(barrier, len(partners) + 2 * core)

    rows_in = wg.shape[2]

    q_cols, kv_cols = pl.ds(0, hs), pl.ds(hs, 2 * hs)

    def gather(tag, cols, direct):
        part = (rows_in - direct) // 2
        ringed = Gather(
            "w" + tag, copies, me, "x",
            (lambda e: w_hbm.at[e, pl.ds(direct, 2 * part), cols]), wg,
            lambda ref, rel, e, which: ref.at[rel, e, pl.ds(direct + which * part, part), cols],
            lambda ref, rel, e: ref.at[rel, e, pl.ds(direct, 2 * part), cols],
        )
        return ringed, Direct("d" + tag, copies, me, w_hbm, wg, direct, cols)

    wk, dk = gather("k", kv_cols, rows_in * 5 // 12)
    wq, dq = gather("q", q_cols, rows_in // 2)
    wk.ring_start()
    gate_copy = pltpu.make_async_copy(mod_hbm.at[gate_part], mod.at[gate_part], local.at[22])
    gate_copy.start()
    own_w = pltpu.make_async_copy(w_hbm, wg.at[OWN], local.at[0])
    own_w.start()
    own_wo = pltpu.make_async_copy(wo_hbm, wo.at[OWN], local.at[1])
    own_wo.start()
    first, second = pl.ds(0, rows), pl.ds(rows, rows)
    copies.start("zr0", xg.at[OWN, first], xg.at[LEFT, first], me.to(z=1))
    copies.start("zl1", xg.at[OWN, second], xg.at[RIGHT, second], me.to(z=-1))
    copies.start("zr1", xg.at[OWN, second], xg.at[LEFT, second], me.to(z=1))
    copies.start("zl0", xg.at[OWN, first], xg.at[RIGHT, first], me.to(z=-1))
    copies.start("qs", queue_hbm.at[1 - core], qb.at[core], me.to(flip=True))

    wk.ring_relay()
    dk.start()
    wq.ring_start()
    copies.got("zr0")
    copies.start("zrr", xg.at[LEFT, first], xg.at[OPP, first], me.to(z=1))
    copies.got("zl1")
    copies.start("zll", xg.at[RIGHT, second], xg.at[OPP, second], me.to(z=-1))
    outs.ring_start()
    wk.ring_end()
    wk.y_relay(LEFT)
    wk.y_relay(RIGHT)
    dk.relay()
    wq.ring_relay()
    dq.start()
    wk.y_relay(OPP)
    wk.y_end(LEFT)
    wk.y_end(RIGHT)
    dk.end()
    gains_copy.wait()
    q_gain = gains_ref[0:1, :] * f32(1.4426950408889634 / hs**0.5)
    k_gain = gains_ref[1:2, :]
    groups = (pl.ds(0, NZ - 1), pl.ds(NZ - 1, 1))
    sizes = (NZ - 1, 1)

    def send_rows(tag, sent, home, rel, which):
        if rel == OWN:
            copies.start(
                "a" + tag, sent.at[OWN, 1 - core, which], home.at[core, which], me.to(flip=True)
            )
            home[core, which] = sent[OWN, core, which]
            return
        spot = home.at[back[rel] * 2 + core, which]
        copies.start("a" + tag, sent.at[rel, core, which], spot, me.to(x=shift[rel]))
        copies.start(
            "b" + tag, sent.at[rel, 1 - core, which], spot, me.to(x=shift[rel], flip=True)
        )

    def project_kv(rel, group):
        which, count = groups[group], sizes[group]
        xs = xg[which].reshape(count * 2 * rows, width)
        w = wg[rel, :, :, hs:].reshape(width, 2 * hs)
        kv = jnp.dot(xs, w, preferred_element_type=f32)
        k = rms_scale(kv[:, :hs], k_gain)
        out = jnp.concatenate([k, kv[:, hs:]], axis=-1).astype(bf16)
        out = out.reshape(count, 2, rows, 2 * hs)
        for slot in range(2):
            sbk[rel, slot, which] = out[:, slot]
        send_rows(f"k{rel}{group}", sbk, rbk, rel, which)

    def project_q(rel):
        xs = xg[...].reshape(NZ * 2 * rows, width)
        w = wg[rel, :, :, :hs].reshape(width, hs)
        q = rms_scale(jnp.dot(xs, w, preferred_element_type=f32), q_gain)
        out = q.astype(bf16).reshape(NZ, 2, rows, hs)
        for slot in range(2):
            sbq[rel, slot] = out[:, slot]
        send_rows(f"q{rel}", sbq, rbq, rel, pl.ds(0, NZ))

    def share(rel, group):
        n = f"{rel}{group}"
        copies.got("ak" + n)
        if rel != OWN:
            copies.got("bk" + n)
        spot = OWN if rel == OWN else back[rel]
        pair = pl.ds(spot * 2, 2)
        src = rbk.at[pair, groups[group]]
        side = copies.make("kv" + n, src, kvb.at[1, pair, groups[group]], (beside, me.head, 1 - core))

        @pl.when(has_beside)
        def _():
            side.start()

        copies.start("ks" + n, src, kvb.at[0, pair, groups[group]], me.to(flip=True))

    own_w.wait()
    copies.got("zr1", "zl0")
    project_kv(OWN, 0)
    wq.ring_end()
    wk.done(LEFT)
    dk.got("s1")
    project_kv(LEFT, 0)
    wk.done(RIGHT)
    dk.got("s2")
    project_kv(RIGHT, 0)
    outs.ring_relay()
    share(OWN, 0)
    wk.y_end(OPP)
    wq.y_relay(LEFT)
    dq.relay()
    wk.done(OPP)
    dk.got("s3")
    project_kv(OPP, 0)
    wq.y_relay(RIGHT)
    share(LEFT, 0)
    share(RIGHT, 0)
    wq.y_relay(OPP)
    wq.y_end(LEFT)
    copies.got("zrr", "zll")
    for rel in (OPP, LEFT, RIGHT, OWN):
        project_kv(rel, 1)
    share(OPP, 0)
    outs.ring_last()
    dq.end()
    wq.y_end(RIGHT)
    wq.y_end(OPP)
    project_q(OWN)
    wq.done(LEFT)
    dq.got("s1")
    project_q(LEFT)
    share(LEFT, 1)
    wq.done(RIGHT)
    dq.got("s2")
    project_q(RIGHT)
    share(OPP, 1)
    share(RIGHT, 1)
    share(OWN, 1)
    wq.done(OPP)
    dq.got("s3")
    project_q(OPP)
    outs.ring_end()
    names = [f"{rel}{group}" for rel in range(4) for group in range(2)]

    ones = jnp.ones((keys, hs), bf16)

    def take(which, kv):
        kt[which] = kv[:, :hs].T
        vx[which, :, :hs] = kv[:, hs:]
        vx[which, :, hs:] = ones

    block = 2 * tokens

    def queries(i):
        return rbq[pl.ds(2 * i, 2)].reshape(block, hs)

    def first_part(rx):
        q = queries(rx)
        scores = [jnp.dot(q, kt[j], preferred_element_type=f32) for j in range(2)]
        peak = jnp.maximum(
            jnp.max(scores[0], axis=-1, keepdims=True), jnp.max(scores[1], axis=-1, keepdims=True)
        )
        total = jnp.zeros((block, 2 * hs), f32)
        for j in range(2):
            p = jnp.exp2(scores[j] - peak).astype(bf16)
            total += jnp.dot(p, vx[j], preferred_element_type=f32)
        oa[rx] = total
        top[rx] = jnp.broadcast_to(peak, (block, hs))

    def attend(rx):
        @pl.when(has_beside)
        def _():
            s = jnp.dot(queries(rx), kt[2], preferred_element_type=f32)
            old = top[rx][:, :1]
            peak = jnp.maximum(old, jnp.max(s, axis=-1, keepdims=True))
            p = jnp.exp2(s - peak).astype(bf16)
            oa[rx] = oa[rx] * jnp.exp2(old - peak) + jnp.dot(
                p, vx[2], preferred_element_type=f32
            )

        o = oa[rx]
        attn = (o[:, :hs] / o[:, hs:]).astype(bf16).reshape(2, NZ, rows, hs)
        attn_g[rx, OWN] = attn[:, OWN].reshape(2 * rows, hs)
        for rz in (LEFT, RIGHT, OPP):
            attn_s[rx, rz] = attn[:, rz].reshape(2 * rows, hs)
            copies.start(
                f"t{rx}{rz}", attn_s.at[rx, rz], attn_g.at[rx, back[rz]], me.to(z=shift[rz])
            )

    def contribution(rx):
        copies.got(*[f"t{rx}{rz}" for rz in (LEFT, RIGHT, OPP)])
        a = jnp.concatenate([attn_g[rx, rz] for rz in range(NZ)], axis=-1)
        return jnp.dot(a, wo[...].reshape(NZ * hs, width), preferred_element_type=f32)

    take(0, rbk[...].reshape(keys, 2 * hs))
    copies.got(*["ks" + n for n in names])
    take(1, kvb[0].reshape(keys, 2 * hs))
    copies.got("aq0")
    for rel in (LEFT, RIGHT, OPP):
        copies.got(f"aq{rel}", f"bq{rel}")
    first_part(OPP)
    outs.y_relay(LEFT)
    outs.y_relay(RIGHT)
    first_part(RIGHT)
    outs.y_relay(OPP)

    @pl.when(has_beside)
    def _():
        for n in names:
            copies.got("kv" + n)
        take(2, kvb[1].reshape(keys, 2 * hs))

    attend(OPP)
    attend(RIGHT)
    for rel in (LEFT, RIGHT, OPP):
        outs.y_end(rel)
    first_part(LEFT)
    attend(LEFT)
    own_wo.wait()
    for rel in (LEFT, RIGHT, OPP):
        outs.done(rel)

    pieces = PIECES
    sub = half // pieces
    p = contribution(OPP).astype(bf16)
    for j in range(pieces):
        po[j] = p[:, j * sub : (j + 1) * sub]
        po[pieces + j] = p[:, half + j * sub : half + (j + 1) * sub]
        copies.start(f"rl{j}", po.at[j], rl.at[j], me.to(x=1))
        copies.start(f"rr{j}", po.at[pieces + j], rr.at[j], me.to(x=-1))
    first_part(OWN)
    attend(OWN)

    right = contribution(RIGHT)
    for j in range(pieces):
        pr_s[pieces + j] = right[:, half + j * sub : half + (j + 1) * sub].astype(bf16)
        copies.start(f"fl{pieces + j}", pr_s.at[pieces + j], fl.at[pieces + j], me.to(x=1))
    left = contribution(LEFT)
    for j in range(pieces):
        pl_s[j] = left[:, j * sub : (j + 1) * sub].astype(bf16)
        copies.start(f"fr{j}", pl_s.at[j], fr.at[j], me.to(x=-1))
    for j in range(pieces):
        copies.got(f"rl{j}")
        pr_s[j] = (right[:, j * sub : (j + 1) * sub] + rl[j].astype(f32)).astype(bf16)
        copies.start(f"fl{j}", pr_s.at[j], fl.at[j], me.to(x=1))
        copies.got(f"rr{j}")
        pl_s[pieces + j] = (
            left[:, half + j * sub : half + (j + 1) * sub] + rr[j].astype(f32)
        ).astype(bf16)
        copies.start(f"fr{pieces + j}", pl_s.at[pieces + j], fr.at[pieces + j], me.to(x=-1))

    p = contribution(OWN)
    copies.got("qs")
    qb[core] = queue_ref[core]
    gate_copy.wait()
    gate = mod[2, pl.ds(steps_ref[core], 1), :]
    sends_on = jnp.logical_and(core == 1, frame < frames - 1)
    near, next0, next1, kept = {}, {}, {}, {}
    noise_copy = pltpu.make_async_copy(noise_hbm, out_hbm.at[0], local.at[9])

    @pl.when(frame == 0)
    def _():
        noise_copy.start()

    for j in range(pieces):
        copies.got(f"fl{j}", f"fr{j}", f"fl{pieces + j}", f"fr{pieces + j}")
        for h in (j, pieces + j):
            cols = slice(h * sub, (h + 1) * sub)
            proj = p[:, cols] + fl[h].astype(f32) + fr[h].astype(f32)
            for tok in range(2):
                ob[h, tok] = (
                    qb[tok, :, cols].astype(f32)
                    + gate[:, cols] * proj[tok * rows : (tok + 1) * rows]
                ).astype(bf16)
        for h in (j, pieces + j):
            cols = pl.ds(h * sub, sub)
            kept[h] = pltpu.make_async_copy(ob.at[h, 0], out_hbm.at[1, :, cols], local.at[32 + h])
            near[h] = copies.make(f"o{h}", ob.at[h, 1], ou.at[1, h], me.to(flip=True))
            next0[h] = copies.make(f"n{h}", ob.at[h, 0], ou.at[0, h], (after, me.head, 0))
            next1[h] = pltpu.make_async_remote_copy(
                src_ref=ob.at[h, 1], dst_ref=ou.at[0, h],
                send_sem=local.at[24 + h], recv_sem=recv.at[copies.count - 1],
                device_id=(after, me.head, 1), device_id_type=MESH,
            )

        @pl.when(core == 0)
        def _():
            for h in (j, pieces + j):
                near[h].start()
                kept[h].start()

        @pl.when(sends_on)
        def _():
            for h in (j, pieces + j):
                next0[h].start()
                next1[h].start()

    def keep(slot, h):
        cols = pl.ds(h * sub, sub)
        return pltpu.make_async_copy(
            ou.at[slot, h], out_hbm.at[slot, :, cols], local.at[40 + 2 * pieces * slot + h]
        )

    @pl.when(core == 1)
    def _():
        for h in range(2 * pieces):
            near[h].wait_recv()
            keep(1, h).start()

    @pl.when(frame > 0)
    def _():
        for h in range(2 * pieces):
            next0[h].wait_recv()
            keep(0, h).start()

    @pl.when(core == 0)
    def _():
        for h in range(2 * pieces):
            near[h].wait_send()
            kept[h].wait()

    @pl.when(core == 1)
    def _():
        for h in range(2 * pieces):
            keep(1, h).wait()

    @pl.when(frame > 0)
    def _():
        for h in range(2 * pieces):
            keep(0, h).wait()

    @pl.when(frame == 0)
    def _():
        noise_copy.wait()

    @pl.when(sends_on)
    def _():
        for h in range(2 * pieces):
            next0[h].wait_send()
            next1[h].wait_send()

    @pl.when(has_beside)
    def _():
        for n in names:
            copies.all["kv" + n].wait_send()

    copies.sent(skip=[f"{t}{h}" for t in "on" for h in range(2 * pieces)] + ["kv" + n for n in names])


def body(queue, timesteps, mod_table, w_qkv, norm_gains, w_out, noise_frame):
    slots, rows, width = queue.shape
    hs = w_out.shape[1]
    bf16, f32 = jnp.bfloat16, jnp.float32
    hbm = pl.BlockSpec(memory_space=pl.ANY)
    smem = pl.BlockSpec(memory_space=pltpu.SMEM)
    tokens = NZ * rows
    keys = NX * 2 * tokens
    eighth = width // 8
    half = width // 2
    sub = half // PIECES
    table = jnp.transpose(mod_table, (1, 0, 2))
    return pl.pallas_call(
        block_kernel,
        out_shape=jax.ShapeDtypeStruct(queue.shape, bf16),
        in_specs=[smem] + [hbm] * 6,
        out_specs=hbm,
        scratch_shapes=[
            pltpu.VMEM(table.shape, f32),
            pltpu.VMEM(queue.shape, bf16),
            pltpu.VMEM(norm_gains.shape, f32),
            pltpu.VMEM((NZ, 2 * rows, width), bf16),
            pltpu.VMEM((NX, 8, eighth, 3 * hs), bf16),
            pltpu.VMEM((NX, 2, NZ, rows, 2 * hs), bf16),
            pltpu.VMEM((NX * 2, NZ, rows, 2 * hs), bf16),
            pltpu.VMEM((NX, 2, NZ, rows, hs), bf16),
            pltpu.VMEM((NX * 2, NZ, rows, hs), bf16),
            pltpu.VMEM((2, NX * 2, NZ, rows, 2 * hs), bf16),
            pltpu.VMEM((3, hs, keys), bf16),
            pltpu.VMEM((3, keys, 2 * hs), bf16),
            pltpu.VMEM((NX, 2 * tokens, 2 * hs), f32),
            pltpu.VMEM((NX, 2 * tokens, hs), f32),
            pltpu.VMEM((NX, NZ, 2 * rows, hs), bf16),
            pltpu.VMEM((NX, NZ, 2 * rows, hs), bf16),
            pltpu.VMEM((NZ, 8, hs // 8, width), bf16),
            pltpu.VMEM((2 * PIECES, 2 * rows, sub), bf16),
            pltpu.VMEM((2 * PIECES, 2 * rows, sub), bf16),
            pltpu.VMEM((2 * PIECES, 2 * rows, sub), bf16),
            pltpu.VMEM((PIECES, 2 * rows, sub), bf16),
            pltpu.VMEM((PIECES, 2 * rows, sub), bf16),
            pltpu.VMEM((2 * PIECES, 2 * rows, sub), bf16),
            pltpu.VMEM((2 * PIECES, 2 * rows, sub), bf16),
            pltpu.VMEM((2, rows, width), bf16),
            pltpu.VMEM((2 * PIECES, 2, rows, sub), bf16),
            pltpu.VMEM((2, 2 * PIECES, rows, sub), bf16),
            pltpu.SemaphoreType.DMA((56,)),
            pltpu.SemaphoreType.DMA((224,)),
            pltpu.SemaphoreType.DMA((224,)),
        ],
        compiler_params=pltpu.CompilerParams(
            collective_id=0, has_side_effects=True, vmem_limit_bytes=56 * 1024 * 1024
        ),
        name="block",
    )(
        timesteps, table, queue, noise_frame, norm_gains,
        w_qkv.reshape(8, eighth, 3 * hs), w_out.reshape(8, hs // 8, width),
    )


def solution(mesh):
    return jax.shard_map(
        body,
        mesh=mesh,
        in_specs=(
            P("frame", ("head", "tok"), None),
            P("frame"),
            P(),
            P(None, "head", None),
            P(),
            P("head", None, None),
            P(("head", "tok"), None),
        ),
        out_specs=P("frame", ("head", "tok"), None),
        check_vma=False,
    )
```
